128 devices in a mesh: row: 8 (over z_lo, y), col: 16 (over z_hi, x, core).
Axes of the slice: x: 4, y: 4, z: 4 (z_hi: 2, z_lo: 2; z = z_hi * 2 + z_lo), core: 2. Of those that a mesh axis runs over, the one named last changes fastest.
Arguments:
- records: bfloat16 [2048, 19200], P(None, ('row', 'col')), may hold values from -40 to 40
- assignment: int32 [2048], replicated, may hold values from 0 to 2047, each once
- channel_flags: int32 [32, 2048], replicated, may hold values from 0 to 1, as said below
Outputs:
- correlations: bfloat16 [2048, 2048, 256], P('row', 'col')
The draws below stay inside these ranges and needn't reach their ends.
Inputs may be any that keep to these rules, and one draw needn't show every extreme that they name: `channel_flags`: exactly 16 channels are bad in every window.
All inputs are finite; a program needn't handle non-finite values.
Results may differ from the reference program's by a relative error of at most 0.0066.
Values may be sent and summed in bfloat16 or wider, within the bound.
No kernel may reach another device: no remote copies, remote signals or barrier semaphores. Data moves between devices by JAX's collectives and lax.ppermute only.
A program may use at most 192 MiB of HBM per device.

```python
import math
import jax
import jax.numpy as jnp
from jax import lax

CHANNELS = 2048
SAMPLES = 600
NFFT = 1024
FIRST_BIN = 10
BINS = 256
MAX_LAG = 128
SMOOTH_HALF = 4
WINDOWS = 32
GROUP_CHANS = 16
DEAD_CHANS = 16
N_ROW = 8
N_COL = 16


def draw_records(key, part):
    key = jax.random.fold_in(key, 11)
    scale_key, noise_key = jax.random.split(key, 2)
    factors = jnp.exp(jax.random.uniform(scale_key, (CHANNELS, WINDOWS), jnp.float32, 0.0, math.log(10.0)))
    base = jax.random.truncated_normal(noise_key, -4.0, 4.0, (CHANNELS, WINDOWS * SAMPLES), jnp.float32)
    values = jnp.repeat(factors, SAMPLES, axis=1) * base
    return jnp.clip(values, -40.0, 40.0).astype(jnp.bfloat16)


def draw_channel_flags(key, part):
    key = jax.random.fold_in(key, 23)
    flag_key, pick_key = jax.random.split(key, 2)
    good = (jax.random.randint(flag_key, (WINDOWS, CHANNELS), 0, 4) < 3).astype(jnp.int32)
    order = jax.random.permutation(pick_key, CHANNELS)
    alive = jnp.ones((CHANNELS,), jnp.int32).at[order[:DEAD_CHANS]].set(0)
    return good * alive[None, :]


def setup_inputs(seed: int = 0) -> dict:
    splits = jax.random.split(jax.random.key(seed), 4)
    records = draw_records(jax.random.fold_in(splits[3], 71), 0)
    assignment = jax.random.permutation(splits[1], CHANNELS).astype(jnp.int32)
    channel_flags = draw_channel_flags(jax.random.fold_in(splits[3], 71), 0)
    return {"records": records, "assignment": assignment, "channel_flags": channel_flags}


water_frac = 0.1

def forward_table():
    sample_idx = jnp.arange(SAMPLES, dtype=jnp.int32)
    band_bins = FIRST_BIN + jnp.arange(BINS, dtype=jnp.int32)
    phase = sample_idx[:, None] * band_bins[None, :] % NFFT
    angle = 2.0 * math.pi / NFFT * phase.astype(jnp.float32)
    return jnp.concatenate([jnp.cos(angle), -jnp.sin(angle)], axis=1).astype(jnp.bfloat16)

def inverse_table():
    band_bins = FIRST_BIN + jnp.arange(BINS, dtype=jnp.int32)
    lag_values = jnp.arange(2 * MAX_LAG, dtype=jnp.int32) - MAX_LAG
    phase = band_bins[:, None] * lag_values[None, :] % NFFT
    angle = 2.0 * math.pi / NFFT * phase.astype(jnp.float32)
    return jnp.concatenate([jnp.cos(angle), -jnp.sin(angle)], axis=0).astype(jnp.bfloat16)

def smooth_bins(spectral_power):
    padded = jnp.pad(spectral_power, ((0, 0), (0, 0), (SMOOTH_HALF, SMOOTH_HALF)))
    total = padded[..., 0:BINS]
    for offset in range(1, 2 * SMOOTH_HALF + 1):
        total = total + padded[..., offset:offset + BINS]
    return total / (2 * SMOOTH_HALF + 1)

def whiten(samples, keep_flags):
    shaped = samples.reshape(samples.shape[0], WINDOWS, SAMPLES).astype(jnp.float32)
    spectrum = jnp.einsum('nws,sf->nwf', shaped, forward_table().astype(jnp.float32))
    real_part = spectrum[..., :BINS]
    imag_part = spectrum[..., BINS:]
    spectral_power = real_part * real_part + imag_part * imag_part
    smoothed = smooth_bins(spectral_power)
    water_level = lax.optimization_barrier(jnp.mean(spectral_power, axis=-1, keepdims=True))
    inverse_amp = lax.rsqrt(smoothed + water_frac * water_level + 1e-06) * jnp.transpose(keep_flags)[:, :, None]
    return (spectrum * jnp.concatenate([inverse_amp, inverse_amp], axis=-1)).astype(jnp.bfloat16)

def make_paired(second_white):
    pair_cols = second_white.shape[0]
    quads = second_white.reshape(pair_cols, WINDOWS, 2, BINS)
    swapped = jnp.stack([-quads[:, :, 1], quads[:, :, 0]], axis=2)
    return jnp.stack([quads, swapped], axis=1).reshape(pair_cols, 2, 2 * WINDOWS, BINS)

def pair_rows(white_rows, paired, pair_scale):
    row_total = white_rows.shape[0]
    pair_cols = paired.shape[0]
    flat_rows = white_rows.reshape(row_total, 2 * WINDOWS, BINS).astype(jnp.float32)
    cross_spec = jnp.einsum('pxk,qyxk->pqyk', flat_rows, paired.astype(jnp.float32))
    stacked = (cross_spec * pair_scale[:, :, None, None]).astype(jnp.bfloat16)
    stacked = stacked.reshape(row_total * pair_cols, 2 * BINS).astype(jnp.float32)
    lagged = jnp.dot(stacked, inverse_table().astype(jnp.float32)) * (1.0 / math.sqrt(BINS))
    return lagged.astype(jnp.bfloat16).reshape(row_total, pair_cols, 2 * MAX_LAG)

def reference(records, assignment, channel_flags):
    flags = channel_flags.astype(jnp.float32)
    whitened = whiten(records, flags)
    col_order = jnp.transpose(assignment.reshape(N_ROW, N_COL, GROUP_CHANS), (1, 0, 2)).reshape(-1)
    first_white = jnp.take(whitened, assignment, axis=0)
    second_white = jnp.take(whitened, col_order, axis=0)
    shared = jnp.dot(jnp.transpose(jnp.take(flags, assignment, axis=1)), jnp.take(flags, col_order, axis=1), precision=lax.Precision.HIGHEST)
    pair_scale = lax.rsqrt(jnp.maximum(shared, 1.0))
    paired = make_paired(second_white)
    blocks_count = CHANNELS // 32
    row_blocks = first_white.reshape(blocks_count, 32, WINDOWS, 2 * BINS)
    scale_blocks = pair_scale.reshape(blocks_count, 32, CHANNELS)
    result = lax.map(lambda member_pair: pair_rows(member_pair[0], paired, member_pair[1]), (row_blocks, scale_blocks))
    return result.reshape(CHANNELS, CHANNELS, 2 * MAX_LAG)
```

```python
import math

import jax
import jax.numpy as jnp
import numpy as np
from jax import lax
from jax.experimental import pallas as pl
from jax.experimental.pallas import tpu as pltpu
from jax.sharding import PartitionSpec as P

SAMPLES = 600
NFFT = 1024
FIRST_BIN = 10
BINS = 256
MAX_LAG = 128
WINDOWS = 32
CHANS = 2048
GROUP = 16
SLICE = 150
QUARTERS = 4
KGS = 64
PITCH = 264

f32 = jnp.float32
bf16 = jnp.bfloat16
vmem = pl.BlockSpec(memory_space=pltpu.VMEM)
smem = pl.BlockSpec(memory_space=pltpu.SMEM)
anym = pl.BlockSpec(memory_space=pl.ANY)


def forward_table():
    phase = (FIRST_BIN + np.arange(BINS))[None, :] * np.arange(SAMPLES)[:, None] % NFFT
    angle = 2.0 * math.pi / NFFT * phase
    table = np.concatenate([np.cos(angle), -np.sin(angle)], axis=1)
    return jnp.asarray(table.reshape(QUARTERS, SLICE, 2 * BINS), bf16)


def lag_table():
    phase = (FIRST_BIN + np.arange(BINS))[None, :] * (np.arange(2 * MAX_LAG) - MAX_LAG)[:, None] % NFFT
    angle = 2.0 * math.pi / NFFT * phase
    table = np.concatenate([np.cos(angle), -np.sin(angle)], axis=1)
    return jnp.asarray(jnp.asarray(table, bf16).astype(f32) / math.sqrt(BINS), bf16)


def order_channels(records_t, assignment):
    block = 512

    def kernel(assign_ref, rec_ref, out_ref, turn_ref):
        chan = lax.broadcasted_iota(jnp.int32, (CHANS, block), 0)
        onehot = (chan == assign_ref[...]).astype(f32).astype(bf16)
        turn_ref[0:SLICE, :] = jnp.dot(rec_ref[...], onehot, preferred_element_type=f32)
        out_ref[...] = turn_ref[...].T[:, :SLICE].astype(bf16)

    return pl.pallas_call(
        kernel,
        out_shape=jax.ShapeDtypeStruct((CHANS, SLICE), bf16),
        grid=(CHANS // block,),
        in_specs=[
            pl.BlockSpec((1, block), lambda i: (0, i)),
            pl.BlockSpec((SLICE, CHANS), lambda i: (0, 0)),
        ],
        out_specs=pl.BlockSpec((block, SLICE), lambda i: (i, 0)),
        scratch_shapes=[pltpu.VMEM((256, block), f32)],
        compiler_params=pltpu.CompilerParams(vmem_limit_bytes=40 * 2**20),
    )(assignment.reshape(1, CHANS), records_t)


def whiten(slices, keep, table):
    def kernel(x_ref, keep_ref, f_ref, out_ref, z0, z1, z2, z3, turn_ref):
        zs = [z0, z1, z2, z3]
        spec = None
        for quarter in range(QUARTERS):
            rows = jnp.concatenate([x_ref[QUARTERS * w + quarter] for w in range(WINDOWS)], axis=0)
            part = jnp.dot(rows, f_ref[quarter], preferred_element_type=f32)
            spec = part if spec is None else spec + part
        re, im = spec[:, :BINS], spec[:, BINS:]
        power = re * re + im * im
        water = jnp.mean(power, axis=1, keepdims=True)
        padded = jnp.concatenate([power, jnp.zeros((512, 128), f32)], axis=1)
        total = padded + pltpu.roll(padded, 1, 1)
        total = total + pltpu.roll(total, 2, 1)
        total = total + pltpu.roll(total, 4, 1)
        total = total + pltpu.roll(padded, 8, 1)
        smooth = pltpu.roll(total, 384 - 4, 1)[:, :BINS]
        amp = lax.rsqrt(smooth / 9.0 + 0.1 * water + 1e-6) * keep_ref[...]
        for h in range(4):
            zs[h][...] = spec[:, h * 128 : (h + 1) * 128] * amp[:, (h % 2) * 128 : (h % 2) * 128 + 128]
        low = lax.broadcasted_iota(jnp.int32, (WINDOWS, 128), 1) < 64
        for ri in range(2):
            for pair in range(GROUP // 2):
                rows = []
                for h in range(2):
                    first = zs[2 * ri + h][pl.ds(2 * pair, WINDOWS, stride=GROUP), :]
                    second = zs[2 * ri + h][pl.ds(2 * pair + 1, WINDOWS, stride=GROUP), :]
                    rows.append(jnp.where(low, first, pltpu.roll(second, 64, 1)))
                    rows.append(jnp.where(low, pltpu.roll(first, 64, 1), second))
                turned = jnp.concatenate(rows, axis=0).T
                for j in range(2):
                    turn_ref[pl.ds(ri * GROUP + 2 * pair + j, KGS, stride=2 * GROUP), :] = turned[
                        j * KGS : (j + 1) * KGS
                    ]
        out_ref[...] = turn_ref[...].astype(bf16)

    out = pl.pallas_call(
        kernel,
        out_shape=jax.ShapeDtypeStruct((KGS * 2 * GROUP, 128), bf16),
        in_specs=[vmem] * 3,
        out_specs=vmem,
        scratch_shapes=[pltpu.VMEM((512, 128), f32)] * 4 + [pltpu.VMEM((KGS * 2 * GROUP, 128), f32)],
        compiler_params=pltpu.CompilerParams(vmem_limit_bytes=40 * 2**20),
    )(slices, keep, table)
    return out.reshape(KGS, 2, GROUP, 128)


def turn_second(blocks, places):
    flat, kinds = flatten(blocks)

    def kernel(*refs):
        place_ref, out_ref, hold = refs[0], refs[-2], refs[-1]
        for half, parts in enumerate(halves(refs[1:-2], kinds)):

            @pl.loop(0, KGS // 2, unroll=4)
            def _(i):
                kg = half * (KGS // 2) + i
                for ri in range(2):
                    for b, (ref, off) in enumerate(parts):
                        row = pl.multiple_of(place_ref[b] * GROUP, GROUP)
                        hold[kg, ri, pl.ds(row, GROUP), :] = ref[i + off, ri]
                for ri in range(2):
                    out_ref[kg, ri] = hold[kg, ri].T

    return pl.pallas_call(
        kernel,
        out_shape=jax.ShapeDtypeStruct((KGS, 2, 128, 128), bf16),
        in_specs=[smem] + [vmem] * len(flat),
        out_specs=vmem,
        scratch_shapes=[pltpu.VMEM((KGS, 2, 128, 128), bf16)],
        compiler_params=pltpu.CompilerParams(vmem_limit_bytes=40 * 2**20),
        cost_estimate=pl.CostEstimate(flops=4 * 10**9, bytes_accessed=8 * 2**20, transcendentals=0),
    )(places, *flat)


def flatten(blocks):
    flat, kinds = [], []
    for block in blocks:
        kinds.append(len(block))
        flat.extend(block)
    return flat, kinds


def halves(refs, kinds):
    out = [[], []]
    at = 0
    for kind in kinds:
        for half in range(2):
            if kind == 1:
                out[half].append((refs[at], half * (KGS // 2)))
            else:
                out[half].append((refs[at + half], 0))
        at += kind
    return out


def pair_chunk(blocks, places, second, scale, table, result):
    flat, kinds = flatten(blocks)
    count = len(blocks)
    rows = count * GROUP

    def kernel(*refs):
        place_ref, sec_ref, scale_ref, tab_ref = refs[:4]
        firsts = refs[4 : 4 + len(flat)]
        out_hbm, spec_re, spec_im, stage, sems = refs[-5:]
        lane = lax.broadcasted_iota(jnp.int32, (rows, 256), 1) % 128 // 32
        starts = [pl.multiple_of(place_ref[b] * GROUP, GROUP) for b in range(count)]
        scales = jnp.concatenate([scale_ref[pl.ds(s, GROUP), :] for s in starts], axis=0)
        for half, parts in enumerate(halves(firsts, kinds)):

            @pl.loop(0, KGS // 2, unroll=8)
            def _(i):
                kg = half * (KGS // 2) + i
                vr, vi = sec_ref[kg, 0], sec_ref[kg, 1]
                rhs = jnp.concatenate(
                    [jnp.concatenate([vr, -vi], axis=1), jnp.concatenate([vi, vr], axis=1)], axis=0
                )
                lhs = jnp.concatenate(
                    [jnp.concatenate([ref[i + off, ri] for ref, off in parts], axis=0) for ri in range(2)],
                    axis=1,
                )
                lhs = jnp.concatenate(
                    [jnp.where(lane == ki, lhs, jnp.zeros_like(lhs)) for ki in range(4)], axis=0
                )
                cross = jnp.dot(lhs, rhs, preferred_element_type=f32)
                for ki in range(4):
                    part = cross[ki * rows : (ki + 1) * rows]
                    spec_re[pl.ds(ki * KGS + kg, rows, stride=PITCH), :] = part[:, :128] * scales
                    spec_im[pl.ds(ki * KGS + kg, rows, stride=PITCH), :] = part[:, 128:] * scales

        def copy_out(b):
            return pltpu.make_async_copy(
                stage.at[pl.ds(b * GROUP, GROUP)], out_hbm.at[pl.ds(starts[b], GROUP)], sems.at[b]
            )

        for b in range(count):

            @pl.loop(0, GROUP // 2, unroll=8)
            def _(i):
                weights = []
                for j in range(2):
                    at = pl.multiple_of((b * GROUP + 2 * i + j) * PITCH, 8)
                    weights.append(
                        jnp.concatenate(
                            [
                                spec_re[pl.ds(at, BINS), :].astype(bf16),
                                spec_im[pl.ds(at, BINS), :].astype(bf16),
                            ],
                            axis=0,
                        )
                    )
                lagged = jnp.dot(
                    tab_ref[...], jnp.concatenate(weights, axis=1), preferred_element_type=f32
                ).astype(bf16)
                for j in range(2):
                    stage[b * GROUP + 2 * i + j] = lagged[:, j * 128 : (j + 1) * 128].T

            copy_out(b).start()
        for b in range(count):
            copy_out(b).wait()

    ins = [places, second, scale, table, *flat]
    specs = [smem, vmem, vmem, vmem] + [vmem] * len(flat)
    aliases = {}
    if result is not None:
        aliases = {len(ins): 0}
        ins.append(result)
        specs.append(anym)
    return pl.pallas_call(
        kernel,
        out_shape=jax.ShapeDtypeStruct((256, 128, 2 * MAX_LAG), bf16),
        in_specs=specs,
        out_specs=anym,
        scratch_shapes=[
            pltpu.VMEM((rows * PITCH, 128), f32),
            pltpu.VMEM((rows * PITCH, 128), f32),
            pltpu.VMEM((rows, 128, 2 * MAX_LAG), bf16),
            pltpu.SemaphoreType.DMA((count,)),
        ],
        input_output_aliases=aliases,
        compiler_params=pltpu.CompilerParams(vmem_limit_bytes=48 * 2**20),
        cost_estimate=pl.CostEstimate(flops=15 * 10**9, bytes_accessed=10 * 2**20, transcendentals=0),
    )(*ins)


def col_perm(dz, dx, dcore):
    def to(i):
        z, x, core = i // 8, i // 2 % 4, i % 2
        return ((z ^ dz) * 4 + (x + dx) % 4) * 2 + (core ^ dcore)

    return [(i, to(i)) for i in range(16)]


def row_perm(dz, dy):
    return [(i, (i // 4 ^ dz) * 4 + (i % 4 + dy) % 4) for i in range(8)]


def ring_of_four(own, axis, up, down):
    below = lax.ppermute(own, axis, up)
    above = lax.ppermute(own, axis, down)
    half = KGS // 2
    far = [lax.ppermute(below[:half], axis, up), lax.ppermute(above[half:], axis, down)]
    return [own], [below], [above], far


def per_device(records, assignment, channel_flags):
    row = lax.axis_index("row")
    col = lax.axis_index("col")
    layout = assignment.reshape(8, 16, GROUP)
    row_chans = lax.dynamic_index_in_dim(layout, row, 0, keepdims=False).reshape(-1)
    col_chans = lax.dynamic_index_in_dim(layout, col, 1, keepdims=False).reshape(-1)
    own_row = lax.dynamic_index_in_dim(layout, row, 0, keepdims=False)
    own_chans = lax.dynamic_index_in_dim(own_row, col, 0, keepdims=False)

    ordered = order_channels(records.T, assignment)
    slices = lax.all_to_all(
        ordered.reshape(128, GROUP, SLICE), ("row", "col"), split_axis=0, concat_axis=0, tiled=True
    )

    flags = channel_flags.astype(f32)
    row_flags = jnp.take(flags, row_chans, axis=1, mode="clip")
    col_flags = jnp.take(flags, col_chans, axis=1, mode="clip")
    keep = jnp.take(flags, own_chans, axis=1, mode="clip").reshape(WINDOWS * GROUP, 1)
    shared = jnp.dot(jnp.transpose(row_flags), col_flags, precision=lax.Precision.HIGHEST)
    scale = lax.rsqrt(jnp.maximum(shared, 1.0))

    own = whiten(slices, keep, forward_table())

    own_zh = lax.ppermute(own, "col", col_perm(1, 0, 0))
    own_zl = lax.ppermute(own, "row", row_perm(1, 0))
    up_y, down_y = row_perm(0, 1), row_perm(0, -1)
    up_x, down_x = col_perm(0, 1, 0), col_perm(0, -1, 0)
    second = ring_of_four(own, "row", up_y, down_y) + ring_of_four(own_zl, "row", up_y, down_y)
    first = ring_of_four(own, "col", up_x, down_x) + ring_of_four(own_zh, "col", up_x, down_x)
    flip = col_perm(0, 0, 1)
    other = [[lax.ppermute(part, "col", flip) for part in block] for block in first]

    z_lo, y = row // 4, row % 4
    z_hi, x, core = col // 8, col // 2 % 4, col % 2
    steps = (0, -1, 1, 2)
    second_places = jnp.stack([(z_lo ^ dz) * 4 + (y + d) % 4 for dz in range(2) for d in steps])
    turned = turn_second(second, second_places.astype(jnp.int32))
    places = [((z_hi ^ dz) * 4 + (x + d) % 4) * 2 for dz in range(2) for d in steps]

    table = lag_table()
    result = None
    for c in range(4):
        members = (2 * c, 2 * c + 1)
        blocks, spots = [], []
        for m in members:
            blocks += [first[m], other[m]]
            spots += [places[m] + core, places[m] + (core ^ 1)]
        result = pair_chunk(blocks, jnp.stack(spots).astype(jnp.int32), turned, scale, table, result)
    return result


def solution(mesh):
    placed = (P(None, ("row", "col")), P(), P())
    return jax.shard_map(
        per_device, mesh=mesh, in_specs=placed, out_specs=P("row", "col", None), check_vma=False
    )
```

```python
import math

import jax
import jax.numpy as jnp
import numpy as np
from jax import lax
from jax.experimental import pallas as pl
from jax.experimental.pallas import tpu as pltpu
from jax.sharding import PartitionSpec as P

SAMPLES = 600
NFFT = 1024
FIRST_BIN = 10
BINS = 256
MAX_LAG = 128
WINDOWS = 32
CHANS = 2048
GROUP = 16
SLICE = 150
QUARTERS = 4
KGS = 64
PITCH = 264

f32 = jnp.float32
bf16 = jnp.bfloat16
vmem = pl.BlockSpec(memory_space=pltpu.VMEM)
smem = pl.BlockSpec(memory_space=pltpu.SMEM)
anym = pl.BlockSpec(memory_space=pl.ANY)
hbm = pl.BlockSpec(memory_space=pltpu.HBM)


def forward_table():
    phase = (FIRST_BIN + np.arange(BINS))[None, :] * np.arange(SAMPLES)[:, None] % NFFT
    angle = 2.0 * math.pi / NFFT * phase
    table = np.concatenate([np.cos(angle), -np.sin(angle)], axis=1)
    return jnp.asarray(table.reshape(QUARTERS, SLICE, 2 * BINS), bf16)


def lag_table():
    phase = (FIRST_BIN + np.arange(BINS))[None, :] * (np.arange(2 * MAX_LAG) - MAX_LAG)[:, None] % NFFT
    angle = 2.0 * math.pi / NFFT * phase
    table = np.concatenate([np.cos(angle), -np.sin(angle)], axis=1)
    return jnp.asarray(jnp.asarray(table, bf16).astype(f32) / math.sqrt(BINS), bf16)


def order_channels(records_t, assignment):
    block = 512

    def kernel(assign_hbm, rec_hbm, out_ref, assign_ref, rec_ref, turn_ref, sems):
        assign_in = pltpu.make_async_copy(assign_hbm, assign_ref, sems.at[0])
        rec_in = pltpu.make_async_copy(rec_hbm, rec_ref, sems.at[1])
        assign_in.start()
        rec_in.start()
        assign_in.wait()
        chan = lax.broadcasted_iota(jnp.int32, (CHANS, block), 0)
        for n in range(CHANS // block):
            at = slice(n * block, (n + 1) * block)
            onehot = (chan == assign_ref[:, at]).astype(f32).astype(bf16)
            if n == 0:
                rec_in.wait()
            turn_ref[n, 0:SLICE, :] = jnp.dot(rec_ref[...], onehot, preferred_element_type=f32)
            out_ref[at, :] = turn_ref[n].T[:, :SLICE].astype(bf16)

    return pl.pallas_call(
        kernel,
        out_shape=jax.ShapeDtypeStruct((CHANS, SLICE), bf16),
        in_specs=[anym, anym],
        out_specs=vmem,
        scratch_shapes=[
            pltpu.VMEM((1, CHANS), jnp.int32),
            pltpu.VMEM((SLICE, CHANS), bf16),
            pltpu.VMEM((CHANS // block, 256, block), f32),
            pltpu.SemaphoreType.DMA((2,)),
        ],
        compiler_params=pltpu.CompilerParams(vmem_limit_bytes=58 * 2**20),
    )(assignment.reshape(1, CHANS), records_t)


def whiten(slices, keep, table):
    def kernel(x_ref, keep_ref, f_ref, out_ref, again_ref, z0, z1, z2, z3, turn_ref, sem):
        zs = [z0, z1, z2, z3]
        spec = None
        for quarter in range(QUARTERS):
            rows = jnp.concatenate([x_ref[QUARTERS * w + quarter] for w in range(WINDOWS)], axis=0)
            part = jnp.dot(rows, f_ref[quarter], preferred_element_type=f32)
            spec = part if spec is None else spec + part
        re, im = spec[:, :BINS], spec[:, BINS:]
        power = re * re + im * im
        water = jnp.mean(power, axis=1, keepdims=True)
        padded = jnp.concatenate([power, jnp.zeros((512, 128), f32)], axis=1)
        total = padded + pltpu.roll(padded, 1, 1)
        total = total + pltpu.roll(total, 2, 1)
        total = total + pltpu.roll(total, 4, 1)
        total = total + pltpu.roll(padded, 8, 1)
        smooth = pltpu.roll(total, 384 - 4, 1)[:, :BINS]
        amp = lax.rsqrt(smooth / 9.0 + 0.1 * water + 1e-6) * keep_ref[...]
        for h in range(4):
            zs[h][...] = spec[:, h * 128 : (h + 1) * 128] * amp[:, (h % 2) * 128 : (h % 2) * 128 + 128]
        low = lax.broadcasted_iota(jnp.int32, (WINDOWS, 128), 1) < 64
        for ri in range(2):
            for pair in range(GROUP // 2):
                rows = []
                for h in range(2):
                    first = zs[2 * ri + h][pl.ds(2 * pair, WINDOWS, stride=GROUP), :]
                    second = zs[2 * ri + h][pl.ds(2 * pair + 1, WINDOWS, stride=GROUP), :]
                    rows.append(jnp.where(low, first, pltpu.roll(second, 64, 1)))
                    rows.append(jnp.where(low, pltpu.roll(first, 64, 1), second))
                turned = jnp.concatenate(rows, axis=0).T
                for j in range(2):
                    turn_ref[pl.ds(ri * GROUP + 2 * pair + j, KGS, stride=2 * GROUP), :] = turned[
                        j * KGS : (j + 1) * KGS
                    ]
        out_ref[...] = turn_ref[...].astype(bf16)
        copy = pltpu.make_async_copy(out_ref, again_ref, sem)
        copy.start()
        copy.wait()

    outs = pl.pallas_call(
        kernel,
        out_shape=[jax.ShapeDtypeStruct((KGS * 2 * GROUP, 128), bf16)] * 2,
        in_specs=[vmem] * 3,
        out_specs=[vmem, hbm],
        scratch_shapes=[pltpu.VMEM((512, 128), f32)] * 4
        + [pltpu.VMEM((KGS * 2 * GROUP, 128), f32), pltpu.SemaphoreType.DMA],
        compiler_params=pltpu.CompilerParams(vmem_limit_bytes=40 * 2**20),
    )(slices, keep, table)
    return [out.reshape(KGS, 2, GROUP, 128) for out in outs]


def after(arrays, others):
    count = len(arrays)
    return pl.pallas_call(
        lambda *refs: None,
        out_shape=[jax.ShapeDtypeStruct(a.shape, a.dtype) for a in arrays],
        in_specs=[hbm] * (count + len(others)),
        out_specs=[hbm] * count,
        input_output_aliases={n: n for n in range(count)},
        cost_estimate=pl.CostEstimate(flops=0, bytes_accessed=0, transcendentals=0),
    )(*arrays, *others)


def pair_chunk(blocks, places, second, scale, table, result):
    count = len(blocks)
    group = 4
    rows = group * GROUP
    slots = 8

    def kernel(*refs):
        place_ref, scale_ref, tab_ref = refs[:3]
        out_hbm, held, spec_re, spec_im, stage, in_sems, sems = refs[-7:]
        half = KGS // 2

        def copy_in(n, h):
            at = pl.ds(h * half, half)
            return pltpu.make_async_copy(refs[3 + n].at[at], held.at[n, at], in_sems.at[n, h])

        for h in range(2):
            for n in range(8 + group):
                copy_in(n, h).start()
        for n in range(8 + group, 8 + count):
            for h in range(2):
                copy_in(n, h).start()
        seconds = [held.at[b] for b in range(8)]
        firsts = [held.at[8 + b] for b in range(count)]
        lane = lax.broadcasted_iota(jnp.int32, (rows, 256), 1) % 128 // 32
        starts = [pl.multiple_of(place_ref[b] * GROUP, GROUP) for b in range(count)]
        columns = [pl.multiple_of(place_ref[count + b] * GROUP, GROUP) for b in range(8)]

        def copy_out(b):
            return pltpu.make_async_copy(
                stage.at[b % slots], out_hbm.at[pl.ds(starts[b], GROUP)], sems.at[b % slots]
            )

        for base in range(0, count, group):
            members = range(base, base + group)
            scales = jnp.concatenate([scale_ref[pl.ds(starts[b], GROUP), :] for b in members], axis=0)

            def cross_bins(kg):
                vr, vi = [jnp.concatenate([ref[kg, ri] for ref in seconds], axis=0) for ri in range(2)]
                rhs = jnp.concatenate(
                    [jnp.concatenate([vr, vi], axis=1), jnp.concatenate([-vi, vr], axis=1)], axis=0
                )
                lhs = jnp.concatenate(
                    [jnp.concatenate([firsts[b][kg, ri] for b in members], axis=0) for ri in range(2)], axis=1
                )
                lhs = jnp.concatenate([jnp.where(lane == ki, lhs, jnp.zeros_like(lhs)) for ki in range(4)], axis=0)
                cross = lax.dot_general(lhs, rhs, (((1,), (1,)), ((), ())), preferred_element_type=f32)
                for ki in range(4):
                    part = cross[ki * rows : (ki + 1) * rows]
                    spec_re[pl.ds(ki * KGS + kg, rows, stride=PITCH), :] = part[:, :128] * scales
                    spec_im[pl.ds(ki * KGS + kg, rows, stride=PITCH), :] = part[:, 128:] * scales

            for h in range(2):
                for n in range(8 + group) if base == 0 else range(8 + base, 8 + base + group):
                    copy_in(n, h).wait()
                for kg in range(h * half, (h + 1) * half):
                    cross_bins(kg)

            for b in members:
                if b >= slots:
                    copy_out(b - slots).wait()
                for i in range(GROUP // 2):
                    halves = []
                    for ref in (spec_re, spec_im):
                        at = [((b - base) * GROUP + 2 * i + j) * PITCH for j in range(2)]
                        halves.append(
                            jnp.concatenate([ref[pl.ds(a, BINS), :].astype(bf16) for a in at], axis=1)
                        )
                    lagged = lax.dot_general(
                        jnp.concatenate(halves, axis=0),
                        tab_ref[...],
                        (((0,), (1,)), ((), ())),
                        preferred_element_type=f32,
                    ).astype(bf16)
                    for j in range(2):
                        for c in range(8):
                            at = j * 128 + c * GROUP
                            stage[b % slots, 2 * i + j, pl.ds(columns[c], GROUP), :] = lagged[at : at + GROUP]
                copy_out(b).start()
        for b in range(max(0, count - slots), count):
            copy_out(b).wait()

    ins = [places, scale, table, *second, *blocks]
    specs = [smem, vmem, vmem] + [hbm] * (8 + count)
    aliases = {}
    if result is not None:
        aliases = {len(ins): 0}
        ins.append(result)
        specs.append(hbm)
    return pl.pallas_call(
        kernel,
        out_shape=jax.ShapeDtypeStruct((256, 128, 2 * MAX_LAG), bf16),
        in_specs=specs,
        out_specs=hbm,
        scratch_shapes=[
            pltpu.VMEM((8 + count, KGS, 2, GROUP, 128), bf16),
            pltpu.VMEM((rows * PITCH, 128), f32),
            pltpu.VMEM((rows * PITCH, 128), f32),
            pltpu.VMEM((slots, GROUP, 128, 2 * MAX_LAG), bf16),
            pltpu.SemaphoreType.DMA((8 + count, 2)),
            pltpu.SemaphoreType.DMA((slots,)),
        ],
        input_output_aliases=aliases,
        compiler_params=pltpu.CompilerParams(vmem_limit_bytes=58 * 2**20),
        cost_estimate=pl.CostEstimate(flops=15 * 10**9, bytes_accessed=10 * 2**20, transcendentals=0),
    )(*ins)


def col_perm(dz, dx, dcore):
    def to(i):
        z, x, core = i // 8, i // 2 % 4, i % 2
        return ((z ^ dz) * 4 + (x + dx) % 4) * 2 + (core ^ dcore)

    return [(i, to(i)) for i in range(16)]


def row_perm(dz, dy):
    return [(i, (i // 4 ^ dz) * 4 + (i % 4 + dy) % 4) for i in range(8)]


def per_device(records, assignment, channel_flags):
    row = lax.axis_index("row")
    col = lax.axis_index("col")
    layout = assignment.reshape(8, 16, GROUP)
    z_lo, y = row // 4, row % 4
    z_hi, x, core = col // 8, col // 2 % 4, col % 2
    steps = (0, -1, 1, 2)
    second_places = [(z_lo ^ dz) * 4 + (y + d) % 4 for dz in range(2) for d in steps]
    row_chans = lax.dynamic_index_in_dim(layout, row, 0, keepdims=False).reshape(-1)
    col_layout = lax.dynamic_index_in_dim(layout, col, 1, keepdims=False)
    col_chans = jnp.take(col_layout, jnp.stack(second_places), axis=0, mode="clip").reshape(-1)
    own_row = lax.dynamic_index_in_dim(layout, row, 0, keepdims=False)
    own_chans = lax.dynamic_index_in_dim(own_row, col, 0, keepdims=False)

    ordered = order_channels(records.T, assignment)
    slices = lax.all_to_all(
        ordered.reshape(128, GROUP, SLICE), ("row", "col"), split_axis=0, concat_axis=0, tiled=True
    )

    flags = channel_flags.astype(f32)
    row_flags = jnp.take(flags, row_chans, axis=1, mode="clip")
    col_flags = jnp.take(flags, col_chans, axis=1, mode="clip")
    keep = jnp.take(flags, own_chans, axis=1, mode="clip").reshape(WINDOWS * GROUP, 1)
    shared = jnp.dot(jnp.transpose(row_flags), col_flags, precision=lax.Precision.HIGHEST)
    scale = lax.rsqrt(jnp.maximum(shared, 1.0))

    places = [
        jnp.stack(
            [((z_hi ^ dz) * 4 + (x + d) % 4) * 2 + (core ^ dc) for dc in range(2) for d in steps] + second_places
        ).astype(jnp.int32)
        for dz in range(2)
    ]
    slices, keep, scale, places = lax.optimization_barrier((slices, keep, scale, places))
    own, again = whiten(slices, keep, forward_table())

    y_up, y_down = row_perm(0, 1), row_perm(0, -1)
    x_up, x_down, flip = col_perm(0, 1, 0), col_perm(0, -1, 0), col_perm(0, 0, 1)

    def along_row(block, perm, name):
        with jax.named_scope(name):
            return lax.ppermute(block, "row", perm)

    def along_col(block, perm, name):
        with jax.named_scope(name):
            return lax.ppermute(block, "col", perm)

    zl = along_row(own, row_perm(1, 0), "zl")
    y_below, y_above = along_row(own, y_up, "y_below"), along_row(own, y_down, "y_above")
    x_below, x_above = along_col(own, x_up, "x_below"), along_col(own, x_down, "x_above")

    (again,) = after([again], [zl, y_below, y_above])
    zl_below, zl_above = along_row(zl, y_up, "zl_below"), along_row(zl, y_down, "zl_above")
    zh = along_col(again, col_perm(1, 0, 0), "zh")
    x_far = along_col(x_below, x_up, "x_far")
    x_far_other = along_col(x_above, col_perm(0, -1, 1), "x_far_other")

    (y_below,) = after([y_below], [zl_below])
    y_far, zl_far = along_row(y_below, y_up, "y_far"), along_row(zl_above, y_down, "zl_far")
    again, x_below, x_above = after([again, x_below, x_above], [zl_below, zl_above, x_far, x_far_other, zh])
    swaps = [along_col(block, flip, "core_swap") for block in (again, x_below, x_above)]
    zh_below, zh_above = along_col(zh, x_up, "zh_below"), along_col(zh, x_down, "zh_above")
    zh_far = along_col(x_far, col_perm(1, 0, 0), "zh_far")
    zh_swaps = [along_col(block, flip, "core_swap") for block in (zh, zh_below, zh_above, zh_far)]

    second = [own, y_below, y_above, y_far, zl, zl_below, zl_above, zl_far]
    table = lag_table()
    result = None
    chunks = (
        [own, x_below, x_above, x_far, *swaps, x_far_other],
        [zh, zh_below, zh_above, zh_far, *zh_swaps],
    )
    for blocks, spots in zip(chunks, places):
        result = pair_chunk(blocks, spots, second, scale, table, result)
    return result


def solution(mesh):
    placed = (P(None, ("row", "col")), P(), P())
    return jax.shard_map(
        per_device, mesh=mesh, in_specs=placed, out_specs=P("row", "col", None), check_vma=False
    )
```

```python
import math

import jax
import jax.numpy as jnp
import numpy as np
from jax import lax
from jax.experimental import pallas as pl
from jax.experimental.pallas import tpu as pltpu
from jax.sharding import PartitionSpec as P

SAMPLES = 600
NFFT = 1024
FIRST_BIN = 10
BINS = 256
MAX_LAG = 128
WINDOWS = 32
CHANS = 2048
GROUP = 16
SLICE = 150
QUARTERS = 4
KGS = 64
PITCH = 264

f32 = jnp.float32
bf16 = jnp.bfloat16
vmem = pl.BlockSpec(memory_space=pltpu.VMEM)
smem = pl.BlockSpec(memory_space=pltpu.SMEM)
anym = pl.BlockSpec(memory_space=pl.ANY)


def forward_table():
    phase = (FIRST_BIN + np.arange(BINS))[None, :] * np.arange(SAMPLES)[:, None] % NFFT
    angle = 2.0 * math.pi / NFFT * phase
    table = np.concatenate([np.cos(angle), -np.sin(angle)], axis=1)
    return jnp.asarray(table.reshape(QUARTERS, SLICE, 2 * BINS), bf16)


def lag_table():
    phase = (FIRST_BIN + np.arange(BINS))[None, :] * (np.arange(2 * MAX_LAG) - MAX_LAG)[:, None] % NFFT
    angle = 2.0 * math.pi / NFFT * phase
    table = np.concatenate([np.cos(angle), -np.sin(angle)], axis=1)
    return jnp.asarray(jnp.asarray(table, bf16).astype(f32) / math.sqrt(BINS), bf16)


def order_channels(records_t, assignment):
    block = 512

    def kernel(assign_hbm, rec_hbm, out_ref, assign_ref, rec_ref, turn_ref, sems):
        assign_in = pltpu.make_async_copy(assign_hbm, assign_ref, sems.at[0])
        rec_in = pltpu.make_async_copy(rec_hbm, rec_ref, sems.at[1])
        assign_in.start()
        rec_in.start()
        assign_in.wait()
        chan = lax.broadcasted_iota(jnp.int32, (CHANS, block), 0)
        for n in range(CHANS // block):
            at = slice(n * block, (n + 1) * block)
            onehot = (chan == assign_ref[:, at]).astype(f32).astype(bf16)
            if n == 0:
                rec_in.wait()
            turn_ref[n, 0:SLICE, :] = jnp.dot(rec_ref[...], onehot, preferred_element_type=f32)
            out_ref[at, :] = turn_ref[n].T[:, :SLICE].astype(bf16)

    return pl.pallas_call(
        kernel,
        out_shape=jax.ShapeDtypeStruct((CHANS, SLICE), bf16),
        in_specs=[anym, anym],
        out_specs=vmem,
        scratch_shapes=[
            pltpu.VMEM((1, CHANS), jnp.int32),
            pltpu.VMEM((SLICE, CHANS), bf16),
            pltpu.VMEM((CHANS // block, 256, block), f32),
            pltpu.SemaphoreType.DMA((2,)),
        ],
        compiler_params=pltpu.CompilerParams(vmem_limit_bytes=58 * 2**20),
    )(assignment.reshape(1, CHANS), records_t)


def whiten(slices, keep, table):
    def kernel(x_ref, keep_ref, f_ref, out_ref, again_ref, z0, z1, z2, z3, turn_ref, sem):
        zs = [z0, z1, z2, z3]
        spec = None
        for quarter in range(QUARTERS):
            rows = jnp.concatenate([x_ref[QUARTERS * w + quarter] for w in range(WINDOWS)], axis=0)
            part = jnp.dot(rows, f_ref[quarter], preferred_element_type=f32)
            spec = part if spec is None else spec + part
        re, im = spec[:, :BINS], spec[:, BINS:]
        power = re * re + im * im
        water = jnp.mean(power, axis=1, keepdims=True)
        padded = jnp.concatenate([power, jnp.zeros((512, 128), f32)], axis=1)
        total = padded + pltpu.roll(padded, 1, 1)
        total = total + pltpu.roll(total, 2, 1)
        total = total + pltpu.roll(total, 4, 1)
        total = total + pltpu.roll(padded, 8, 1)
        smooth = pltpu.roll(total, 384 - 4, 1)[:, :BINS]
        amp = lax.rsqrt(smooth / 9.0 + 0.1 * water + 1e-6) * keep_ref[...]
        for h in range(4):
            zs[h][...] = spec[:, h * 128 : (h + 1) * 128] * amp[:, (h % 2) * 128 : (h % 2) * 128 + 128]
        low = lax.broadcasted_iota(jnp.int32, (WINDOWS, 128), 1) < 64
        for ri in range(2):
            for pair in range(GROUP // 2):
                rows = []
                for h in range(2):
                    first = zs[2 * ri + h][pl.ds(2 * pair, WINDOWS, stride=GROUP), :]
                    second = zs[2 * ri + h][pl.ds(2 * pair + 1, WINDOWS, stride=GROUP), :]
                    rows.append(jnp.where(low, first, pltpu.roll(second, 64, 1)))
                    rows.append(jnp.where(low, pltpu.roll(first, 64, 1), second))
                turned = jnp.concatenate(rows, axis=0).T
                for j in range(2):
                    turn_ref[pl.ds(ri * GROUP + 2 * pair + j, KGS, stride=2 * GROUP), :] = turned[
                        j * KGS : (j + 1) * KGS
                    ]
        out_ref[...] = turn_ref[...].astype(bf16)
        copy = pltpu.make_async_copy(out_ref, again_ref, sem)
        copy.start()
        copy.wait()

    outs = pl.pallas_call(
        kernel,
        out_shape=[jax.ShapeDtypeStruct((KGS * 2 * GROUP, 128), bf16)] * 2,
        in_specs=[vmem] * 3,
        out_specs=[vmem, anym],
        scratch_shapes=[pltpu.VMEM((512, 128), f32)] * 4
        + [pltpu.VMEM((KGS * 2 * GROUP, 128), f32), pltpu.SemaphoreType.DMA],
        compiler_params=pltpu.CompilerParams(vmem_limit_bytes=40 * 2**20),
    )(slices, keep, table)
    return [out.reshape(KGS, 2, GROUP, 128) for out in outs]


def after(arrays, others):
    count = len(arrays)
    return pl.pallas_call(
        lambda *refs: None,
        out_shape=[jax.ShapeDtypeStruct(a.shape, a.dtype) for a in arrays],
        in_specs=[anym] * (count + len(others)),
        out_specs=[anym] * count,
        input_output_aliases={n: n for n in range(count)},
        cost_estimate=pl.CostEstimate(flops=0, bytes_accessed=0, transcendentals=0),
    )(*arrays, *others)


def pair_chunk(blocks, places, second, scale, table, result):
    count = len(blocks)
    group = 4
    rows = group * GROUP
    slots = 8

    def kernel(*refs):
        place_ref, scale_ref, tab_ref = refs[:3]
        out_hbm, held, spec_re, spec_im, stage, in_sems, sems = refs[-7:]
        half = KGS // 2

        def copy_in(n, h):
            at = pl.ds(h * half, half)
            return pltpu.make_async_copy(refs[3 + n].at[at], held.at[n, at], in_sems.at[n, h])

        for h in range(2):
            for n in range(8 + group):
                copy_in(n, h).start()
        for n in range(8 + group, 8 + count):
            for h in range(2):
                copy_in(n, h).start()
        seconds = [held.at[b] for b in range(8)]
        firsts = [held.at[8 + b] for b in range(count)]
        lane = lax.broadcasted_iota(jnp.int32, (rows, 256), 1) % 128 // 32
        starts = [pl.multiple_of(place_ref[b] * GROUP, GROUP) for b in range(count)]
        columns = [pl.multiple_of(place_ref[count + b] * GROUP, GROUP) for b in range(8)]

        def copy_out(b):
            return pltpu.make_async_copy(
                stage.at[b % slots], out_hbm.at[pl.ds(starts[b], GROUP)], sems.at[b % slots]
            )

        for base in range(0, count, group):
            members = range(base, base + group)
            scales = jnp.concatenate([scale_ref[pl.ds(starts[b], GROUP), :] for b in members], axis=0)

            def cross_bins(kg):
                vr, vi = [jnp.concatenate([ref[kg, ri] for ref in seconds], axis=0) for ri in range(2)]
                rhs = jnp.concatenate(
                    [jnp.concatenate([vr, vi], axis=1), jnp.concatenate([-vi, vr], axis=1)], axis=0
                )
                lhs = jnp.concatenate(
                    [jnp.concatenate([firsts[b][kg, ri] for b in members], axis=0) for ri in range(2)], axis=1
                )
                lhs = jnp.concatenate([jnp.where(lane == ki, lhs, jnp.zeros_like(lhs)) for ki in range(4)], axis=0)
                cross = lax.dot_general(lhs, rhs, (((1,), (1,)), ((), ())), preferred_element_type=f32)
                for ki in range(4):
                    part = cross[ki * rows : (ki + 1) * rows]
                    spec_re[pl.ds(ki * KGS + kg, rows, stride=PITCH), :] = part[:, :128] * scales
                    spec_im[pl.ds(ki * KGS + kg, rows, stride=PITCH), :] = part[:, 128:] * scales

            for h in range(2):
                for n in range(8 + group) if base == 0 else range(8 + base, 8 + base + group):
                    copy_in(n, h).wait()
                for kg in range(h * half, (h + 1) * half):
                    cross_bins(kg)

            for b in members:
                if b >= slots:
                    copy_out(b - slots).wait()
                for i in range(GROUP // 2):
                    halves = []
                    for ref in (spec_re, spec_im):
                        at = [((b - base) * GROUP + 2 * i + j) * PITCH for j in range(2)]
                        halves.append(
                            jnp.concatenate([ref[pl.ds(a, BINS), :].astype(bf16) for a in at], axis=1)
                        )
                    lagged = lax.dot_general(
                        jnp.concatenate(halves, axis=0),
                        tab_ref[...],
                        (((0,), (1,)), ((), ())),
                        preferred_element_type=f32,
                    ).astype(bf16)
                    for j in range(2):
                        for c in range(8):
                            at = j * 128 + c * GROUP
                            stage[b % slots, 2 * i + j, pl.ds(columns[c], GROUP), :] = lagged[at : at + GROUP]
                copy_out(b).start()
        for b in range(max(0, count - slots), count):
            copy_out(b).wait()

    ins = [places, scale, table, *second, *blocks]
    specs = [smem, vmem, vmem] + [anym] * (8 + count)
    aliases = {}
    if result is not None:
        aliases = {len(ins): 0}
        ins.append(result)
        specs.append(anym)
    return pl.pallas_call(
        kernel,
        out_shape=jax.ShapeDtypeStruct((256, 128, 2 * MAX_LAG), bf16),
        in_specs=specs,
        out_specs=anym,
        scratch_shapes=[
            pltpu.VMEM((8 + count, KGS, 2, GROUP, 128), bf16),
            pltpu.VMEM((rows * PITCH, 128), f32),
            pltpu.VMEM((rows * PITCH, 128), f32),
            pltpu.VMEM((slots, GROUP, 128, 2 * MAX_LAG), bf16),
            pltpu.SemaphoreType.DMA((8 + count, 2)),
            pltpu.SemaphoreType.DMA((slots,)),
        ],
        input_output_aliases=aliases,
        compiler_params=pltpu.CompilerParams(vmem_limit_bytes=58 * 2**20),
        cost_estimate=pl.CostEstimate(flops=15 * 10**9, bytes_accessed=10 * 2**20, transcendentals=0),
    )(*ins)


def col_perm(dz, dx, dcore):
    def to(i):
        z, x, core = i // 8, i // 2 % 4, i % 2
        return ((z ^ dz) * 4 + (x + dx) % 4) * 2 + (core ^ dcore)

    return [(i, to(i)) for i in range(16)]


def row_perm(dz, dy):
    return [(i, (i // 4 ^ dz) * 4 + (i % 4 + dy) % 4) for i in range(8)]


def per_device(records, assignment, channel_flags):
    row = lax.axis_index("row")
    col = lax.axis_index("col")
    layout = assignment.reshape(8, 16, GROUP)
    z_lo, y = row // 4, row % 4
    z_hi, x, core = col // 8, col // 2 % 4, col % 2
    steps = (0, -1, 1, 2)
    second_places = [(z_lo ^ dz) * 4 + (y + d) % 4 for dz in range(2) for d in steps]
    row_chans = lax.dynamic_index_in_dim(layout, row, 0, keepdims=False).reshape(-1)
    col_layout = lax.dynamic_index_in_dim(layout, col, 1, keepdims=False)
    col_chans = jnp.take(col_layout, jnp.stack(second_places), axis=0, mode="clip").reshape(-1)
    own_row = lax.dynamic_index_in_dim(layout, row, 0, keepdims=False)
    own_chans = lax.dynamic_index_in_dim(own_row, col, 0, keepdims=False)

    ordered = order_channels(records.T, assignment)
    slices = lax.all_to_all(
        ordered.reshape(128, GROUP, SLICE), ("row", "col"), split_axis=0, concat_axis=0, tiled=True
    )

    flags = channel_flags.astype(f32)
    row_flags = jnp.take(flags, row_chans, axis=1, mode="clip")
    col_flags = jnp.take(flags, col_chans, axis=1, mode="clip")
    keep = jnp.take(flags, own_chans, axis=1, mode="clip").reshape(WINDOWS * GROUP, 1)
    shared = jnp.dot(jnp.transpose(row_flags), col_flags, precision=lax.Precision.HIGHEST)
    scale = lax.rsqrt(jnp.maximum(shared, 1.0))

    places = [
        jnp.stack(
            [((z_hi ^ dz) * 4 + (x + d) % 4) * 2 + (core ^ dc) for dc in range(2) for d in steps] + second_places
        ).astype(jnp.int32)
        for dz in range(2)
    ]
    slices, keep, scale, places = lax.optimization_barrier((slices, keep, scale, places))
    own, again = whiten(slices, keep, forward_table())

    y_up, y_down = row_perm(0, 1), row_perm(0, -1)
    x_up, x_down, flip = col_perm(0, 1, 0), col_perm(0, -1, 0), col_perm(0, 0, 1)

    def along_row(block, perm, name):
        with jax.named_scope(name):
            return lax.ppermute(block, "row", perm)

    def along_col(block, perm, name):
        with jax.named_scope(name):
            return lax.ppermute(block, "col", perm)

    zl = along_row(own, row_perm(1, 0), "zl")
    y_below, y_above = along_row(own, y_up, "y_below"), along_row(own, y_down, "y_above")
    x_below, x_above = along_col(own, x_up, "x_below"), along_col(own, x_down, "x_above")

    (again,) = after([again], [zl, y_below, y_above])
    zl_below, zl_above = along_row(zl, y_up, "zl_below"), along_row(zl, y_down, "zl_above")
    zh = along_col(again, col_perm(1, 0, 0), "zh")
    x_far = along_col(x_below, x_up, "x_far")
    x_far_other = along_col(x_above, col_perm(0, -1, 1), "x_far_other")

    (y_below,) = after([y_below], [zl_below])
    y_far, zl_far = along_row(y_below, y_up, "y_far"), along_row(zl_above, y_down, "zl_far")
    zh_below, zh_above = along_col(zh, x_up, "zh_below"), along_col(zh, x_down, "zh_above")
    zh_far = along_col(x_far, col_perm(1, 0, 0), "zh_far")
    again, x_below, x_above = after([again, x_below, x_above], [y_far, zl_far, zh, x_far, x_far_other])
    swaps = [along_col(block, flip, "core_swap") for block in (again, x_below, x_above)]

    second = [own, y_below, y_above, y_far, zl, zl_below, zl_above, zl_far]
    table = lag_table()
    blocks = [own, x_below, x_above, x_far, *swaps, x_far_other]
    result = pair_chunk(blocks, places[0], second, scale, table, None)
    blocks = after([zh, zh_below, zh_above, zh_far], [result])
    blocks = [*blocks, *(along_col(block, flip, "core_swap") for block in blocks)]
    result = pair_chunk(blocks, places[1], second, scale, table, result)
    return result


def solution(mesh):
    placed = (P(None, ("row", "col")), P(), P())
    return jax.shard_map(
        per_device, mesh=mesh, in_specs=placed, out_specs=P("row", "col", None), check_vma=False
    )
```

```python
import math

import jax
import jax.numpy as jnp
import numpy as np
from jax import lax
from jax.experimental import pallas as pl
from jax.experimental.pallas import tpu as pltpu
from jax.sharding import PartitionSpec as P

SAMPLES = 600
NFFT = 1024
FIRST_BIN = 10
BINS = 256
MAX_LAG = 128
WINDOWS = 32
CHANS = 2048
GROUP = 16
SLICE = 150
QUARTERS = 4
KGS = 64
PITCH = 264

f32 = jnp.float32
bf16 = jnp.bfloat16
vmem = pl.BlockSpec(memory_space=pltpu.VMEM)
smem = pl.BlockSpec(memory_space=pltpu.SMEM)
anym = pl.BlockSpec(memory_space=pl.ANY)


def forward_table():
    phase = (FIRST_BIN + np.arange(BINS))[None, :] * np.arange(SAMPLES)[:, None] % NFFT
    angle = 2.0 * math.pi / NFFT * phase
    table = np.concatenate([np.cos(angle), -np.sin(angle)], axis=1)
    return jnp.asarray(table.reshape(QUARTERS, SLICE, 2 * BINS), bf16)


def lag_table():
    phase = (FIRST_BIN + np.arange(BINS))[None, :] * (np.arange(2 * MAX_LAG) - MAX_LAG)[:, None] % NFFT
    angle = 2.0 * math.pi / NFFT * phase
    table = np.concatenate([np.cos(angle), -np.sin(angle)], axis=1)
    return jnp.asarray(jnp.asarray(table, bf16).astype(f32) / math.sqrt(BINS), bf16)


def order_channels(records_t, assignment):
    block = 512

    def kernel(assign_hbm, rec_hbm, out_ref, assign_ref, rec_ref, turn_ref, sems):
        assign_in = pltpu.make_async_copy(assign_hbm, assign_ref, sems.at[0])
        rec_in = pltpu.make_async_copy(rec_hbm, rec_ref, sems.at[1])
        assign_in.start()
        rec_in.start()
        assign_in.wait()
        chan = lax.broadcasted_iota(jnp.int32, (CHANS, block), 0)
        for n in range(CHANS // block):
            at = slice(n * block, (n + 1) * block)
            onehot = (chan == assign_ref[:, at]).astype(f32).astype(bf16)
            if n == 0:
                rec_in.wait()
            turn_ref[n, 0:SLICE, :] = jnp.dot(rec_ref[...], onehot, preferred_element_type=f32)
            out_ref[at, :] = turn_ref[n].T[:, :SLICE].astype(bf16)

    return pl.pallas_call(
        kernel,
        out_shape=jax.ShapeDtypeStruct((CHANS, SLICE), bf16),
        in_specs=[anym, anym],
        out_specs=vmem,
        scratch_shapes=[
            pltpu.VMEM((1, CHANS), jnp.int32),
            pltpu.VMEM((SLICE, CHANS), bf16),
            pltpu.VMEM((CHANS // block, 256, block), f32),
            pltpu.SemaphoreType.DMA((2,)),
        ],
        compiler_params=pltpu.CompilerParams(vmem_limit_bytes=58 * 2**20),
    )(assignment.reshape(1, CHANS), records_t)


def whiten(slices, keep, table):
    def kernel(x_ref, keep_ref, f_ref, out_ref, again_ref, z0, z1, z2, z3, turn_ref, sem):
        zs = [z0, z1, z2, z3]
        spec = None
        for quarter in range(QUARTERS):
            rows = jnp.concatenate([x_ref[QUARTERS * w + quarter] for w in range(WINDOWS)], axis=0)
            part = jnp.dot(rows, f_ref[quarter], preferred_element_type=f32)
            spec = part if spec is None else spec + part
        re, im = spec[:, :BINS], spec[:, BINS:]
        power = re * re + im * im
        water = jnp.mean(power, axis=1, keepdims=True)
        padded = jnp.concatenate([power, jnp.zeros((512, 128), f32)], axis=1)
        total = padded + pltpu.roll(padded, 1, 1)
        total = total + pltpu.roll(total, 2, 1)
        total = total + pltpu.roll(total, 4, 1)
        total = total + pltpu.roll(padded, 8, 1)
        smooth = pltpu.roll(total, 384 - 4, 1)[:, :BINS]
        amp = lax.rsqrt(smooth / 9.0 + 0.1 * water + 1e-6) * keep_ref[...]
        for h in range(4):
            zs[h][...] = spec[:, h * 128 : (h + 1) * 128] * amp[:, (h % 2) * 128 : (h % 2) * 128 + 128]
        low = lax.broadcasted_iota(jnp.int32, (WINDOWS, 128), 1) < 64
        for ri in range(2):
            for pair in range(GROUP // 2):
                rows = []
                for h in range(2):
                    first = zs[2 * ri + h][pl.ds(2 * pair, WINDOWS, stride=GROUP), :]
                    second = zs[2 * ri + h][pl.ds(2 * pair + 1, WINDOWS, stride=GROUP), :]
                    rows.append(jnp.where(low, first, pltpu.roll(second, 64, 1)))
                    rows.append(jnp.where(low, pltpu.roll(first, 64, 1), second))
                turned = jnp.concatenate(rows, axis=0).T
                for j in range(2):
                    turn_ref[pl.ds(ri * GROUP + 2 * pair + j, KGS, stride=2 * GROUP), :] = turned[
                        j * KGS : (j + 1) * KGS
                    ]
        out_ref[...] = turn_ref[...].astype(bf16)
        copy = pltpu.make_async_copy(out_ref, again_ref, sem)
        copy.start()
        copy.wait()

    outs = pl.pallas_call(
        kernel,
        out_shape=[jax.ShapeDtypeStruct((KGS * 2 * GROUP, 128), bf16)] * 2,
        in_specs=[vmem] * 3,
        out_specs=[vmem, anym],
        scratch_shapes=[pltpu.VMEM((512, 128), f32)] * 4
        + [pltpu.VMEM((KGS * 2 * GROUP, 128), f32), pltpu.SemaphoreType.DMA],
        compiler_params=pltpu.CompilerParams(vmem_limit_bytes=40 * 2**20),
    )(slices, keep, table)
    return [out.reshape(KGS, 2, GROUP, 128) for out in outs]


def after(arrays, others):
    count = len(arrays)
    return pl.pallas_call(
        lambda *refs: None,
        out_shape=[jax.ShapeDtypeStruct(a.shape, a.dtype) for a in arrays],
        in_specs=[anym] * (count + len(others)),
        out_specs=[anym] * count,
        input_output_aliases={n: n for n in range(count)},
        cost_estimate=pl.CostEstimate(flops=0, bytes_accessed=0, transcendentals=0),
    )(*arrays, *others)


def pair_chunk(blocks, places, second, scale, table, result):
    count = len(blocks)
    group = 4
    rows = group * GROUP

    def kernel(*refs):
        place_ref, scale_ref, tab_ref = refs[:3]
        out_hbm, held, spec_re, spec_im, stage, in_sems, sems = refs[-7:]
        half = KGS // 2

        def copy_in(n, h):
            at = pl.ds(h * half, half)
            return pltpu.make_async_copy(refs[3 + n].at[at], held.at[n, at], in_sems.at[n, h])

        def copy_out(b):
            at = pl.multiple_of(place_ref[b] * GROUP, GROUP)
            return pltpu.make_async_copy(stage.at[b], out_hbm.at[pl.ds(at, GROUP)], sems.at[b])

        for h in range(2):
            for n in range(8 + group):
                copy_in(n, h).start()
        for n in range(8 + group, 8 + count):
            for h in range(2):
                copy_in(n, h).start()
        lane = lax.broadcasted_iota(jnp.int32, (rows, 256), 1) % 128 // 32
        columns = [pl.multiple_of(place_ref[count + b] * GROUP, GROUP) for b in range(8)]

        @pl.loop(0, count // group)
        def _(turn):
            base = turn * group
            starts = [pl.multiple_of(place_ref[base + b] * GROUP, GROUP) for b in range(group)]
            scales = jnp.concatenate([scale_ref[pl.ds(at, GROUP), :] for at in starts], axis=0)

            @pl.loop(0, 2)
            def _(h):
                @pl.when(turn == 0)
                def _():
                    for n in range(8 + group):
                        copy_in(n, h).wait()

                @pl.when(turn > 0)
                def _():
                    for n in range(8 + group, 8 + count):
                        copy_in(n, h).wait()

                @pl.loop(0, half, unroll=half)
                def _(i):
                    kg = h * half + i
                    vr, vi = [jnp.concatenate([held[b, kg, ri] for b in range(8)], axis=0) for ri in range(2)]
                    rhs = jnp.concatenate(
                        [jnp.concatenate([vr, vi], axis=1), jnp.concatenate([-vi, vr], axis=1)], axis=0
                    )
                    lhs = jnp.concatenate(
                        [
                            jnp.concatenate([held[8 + base + b, kg, ri] for b in range(group)], axis=0)
                            for ri in range(2)
                        ],
                        axis=1,
                    )
                    lhs = jnp.concatenate(
                        [jnp.where(lane == ki, lhs, jnp.zeros_like(lhs)) for ki in range(4)], axis=0
                    )
                    cross = lax.dot_general(lhs, rhs, (((1,), (1,)), ((), ())), preferred_element_type=f32)
                    for ki in range(4):
                        part = cross[ki * rows : (ki + 1) * rows]
                        spec_re[pl.ds(ki * KGS + kg, rows, stride=PITCH), :] = part[:, :128] * scales
                        spec_im[pl.ds(ki * KGS + kg, rows, stride=PITCH), :] = part[:, 128:] * scales

            @pl.loop(0, group // 2)
            def _(couple):
                for i in range(GROUP):
                    b = 2 * couple + i // (GROUP // 2)
                    row = 2 * (i % (GROUP // 2))
                    halves = []
                    for ref in (spec_re, spec_im):
                        at = [pl.multiple_of((b * GROUP + row + j) * PITCH, 8) for j in range(2)]
                        halves.append(
                            jnp.concatenate([ref[pl.ds(a, BINS), :].astype(bf16) for a in at], axis=1)
                        )
                    lagged = lax.dot_general(
                        jnp.concatenate(halves, axis=0),
                        tab_ref[...],
                        (((0,), (1,)), ((), ())),
                        preferred_element_type=f32,
                    ).astype(bf16)
                    for j in range(2):
                        for c in range(8):
                            at = j * 128 + c * GROUP
                            stage[base + b, row + j, pl.ds(columns[c], GROUP), :] = lagged[at : at + GROUP]
                for b in range(2):
                    copy_out(base + 2 * couple + b).start()

        for b in range(count):
            copy_out(b).wait()

    ins = [places, scale, table, *second, *blocks]
    specs = [smem, vmem, vmem] + [anym] * (8 + count)
    aliases = {}
    if result is not None:
        aliases = {len(ins): 0}
        ins.append(result)
        specs.append(anym)
    return pl.pallas_call(
        kernel,
        out_shape=jax.ShapeDtypeStruct((256, 128, 2 * MAX_LAG), bf16),
        in_specs=specs,
        out_specs=anym,
        scratch_shapes=[
            pltpu.VMEM((8 + count, KGS, 2, GROUP, 128), bf16),
            pltpu.VMEM((rows * PITCH, 128), f32),
            pltpu.VMEM((rows * PITCH, 128), f32),
            pltpu.VMEM((count, GROUP, 128, 2 * MAX_LAG), bf16),
            pltpu.SemaphoreType.DMA((8 + count, 2)),
            pltpu.SemaphoreType.DMA((count,)),
        ],
        input_output_aliases=aliases,
        compiler_params=pltpu.CompilerParams(vmem_limit_bytes=58 * 2**20),
        cost_estimate=pl.CostEstimate(flops=15 * 10**9, bytes_accessed=10 * 2**20, transcendentals=0),
    )(*ins)


def col_perm(dz, dx, dcore):
    def to(i):
        z, x, core = i // 8, i // 2 % 4, i % 2
        return ((z ^ dz) * 4 + (x + dx) % 4) * 2 + (core ^ dcore)

    return [(i, to(i)) for i in range(16)]


def row_perm(dz, dy):
    return [(i, (i // 4 ^ dz) * 4 + (i % 4 + dy) % 4) for i in range(8)]


def per_device(records, assignment, channel_flags):
    row = lax.axis_index("row")
    col = lax.axis_index("col")
    layout = assignment.reshape(8, 16, GROUP)
    z_lo, y = row // 4, row % 4
    z_hi, x, core = col // 8, col // 2 % 4, col % 2
    steps = (0, -1, 1, 2)
    second_places = [(z_lo ^ dz) * 4 + (y + d) % 4 for dz in range(2) for d in steps]
    row_chans = lax.dynamic_index_in_dim(layout, row, 0, keepdims=False).reshape(-1)
    col_layout = lax.dynamic_index_in_dim(layout, col, 1, keepdims=False)
    col_chans = jnp.take(col_layout, jnp.stack(second_places), axis=0, mode="clip").reshape(-1)
    own_row = lax.dynamic_index_in_dim(layout, row, 0, keepdims=False)
    own_chans = lax.dynamic_index_in_dim(own_row, col, 0, keepdims=False)

    ordered = order_channels(records.T, assignment)
    slices = lax.all_to_all(
        ordered.reshape(128, GROUP, SLICE), ("row", "col"), split_axis=0, concat_axis=0, tiled=True
    )

    flags = channel_flags.astype(f32)
    row_flags = jnp.take(flags, row_chans, axis=1, mode="clip")
    col_flags = jnp.take(flags, col_chans, axis=1, mode="clip")
    keep = jnp.take(flags, own_chans, axis=1, mode="clip").reshape(WINDOWS * GROUP, 1)
    shared = jnp.dot(jnp.transpose(row_flags), col_flags, precision=lax.Precision.HIGHEST)
    scale = lax.rsqrt(jnp.maximum(shared, 1.0))

    places = [
        jnp.stack(
            [((z_hi ^ dz) * 4 + (x + d) % 4) * 2 + (core ^ dc) for dc in range(2) for d in steps] + second_places
        ).astype(jnp.int32)
        for dz in range(2)
    ]
    slices, keep, scale, places = lax.optimization_barrier((slices, keep, scale, places))
    own, again = whiten(slices, keep, forward_table())

    y_up, y_down = row_perm(0, 1), row_perm(0, -1)
    x_up, x_down, flip = col_perm(0, 1, 0), col_perm(0, -1, 0), col_perm(0, 0, 1)

    def along_row(block, perm, name):
        with jax.named_scope(name):
            return lax.ppermute(block, "row", perm)

    def along_col(block, perm, name):
        with jax.named_scope(name):
            return lax.ppermute(block, "col", perm)

    zl = along_row(own, row_perm(1, 0), "zl")
    y_below, y_above = along_row(own, y_up, "y_below"), along_row(own, y_down, "y_above")
    x_below, x_above = along_col(own, x_up, "x_below"), along_col(own, x_down, "x_above")

    (again,) = after([again], [zl, y_below, y_above])
    zl_below, zl_above = along_row(zl, y_up, "zl_below"), along_row(zl, y_down, "zl_above")
    zh = along_col(again, col_perm(1, 0, 0), "zh")
    x_far = along_col(x_below, x_up, "x_far")
    x_far_other = along_col(x_above, col_perm(0, -1, 1), "x_far_other")

    (y_below,) = after([y_below], [zl_below])
    y_far, zl_far = along_row(y_below, y_up, "y_far"), along_row(zl_above, y_down, "zl_far")
    zh_below, zh_above = along_col(zh, x_up, "zh_below"), along_col(zh, x_down, "zh_above")
    zh_far = along_col(x_far, col_perm(1, 0, 0), "zh_far")
    again, x_below, x_above = after([again, x_below, x_above], [y_far, zl_far, zh, x_far, x_far_other])
    swaps = [along_col(block, flip, "core_swap") for block in (again, x_below, x_above)]

    second = [own, y_below, y_above, y_far, zl, zl_below, zl_above, zl_far]
    table = lag_table()
    blocks = [own, x_below, x_above, x_far, *swaps, x_far_other]
    result = pair_chunk(blocks, places[0], second, scale, table, None)
    blocks = after([zh, zh_below, zh_above, zh_far], [result])
    blocks = [*blocks, *(along_col(block, flip, "core_swap") for block in blocks)]
    result = pair_chunk(blocks, places[1], second, scale, table, result)
    return result


def solution(mesh):
    placed = (P(None, ("row", "col")), P(), P())
    return jax.shard_map(
        per_device, mesh=mesh, in_specs=placed, out_specs=P("row", "col", None), check_vma=False
    )
```

```python
import math

import jax
import jax.numpy as jnp
import numpy as np
from jax import lax
from jax.experimental import pallas as pl
from jax.experimental.pallas import tpu as pltpu
from jax.sharding import PartitionSpec as P

SAMPLES = 600
NFFT = 1024
FIRST_BIN = 10
BINS = 256
MAX_LAG = 128
WINDOWS = 32
CHANS = 2048
GROUP = 16
SLICE = 150
QUARTERS = 4
KGS = 64
PITCH = 264

f32 = jnp.float32
bf16 = jnp.bfloat16
vmem = pl.BlockSpec(memory_space=pltpu.VMEM)
smem = pl.BlockSpec(memory_space=pltpu.SMEM)
anym = pl.BlockSpec(memory_space=pl.ANY)


def forward_table():
    phase = (FIRST_BIN + np.arange(BINS))[None, :] * np.arange(SAMPLES)[:, None] % NFFT
    angle = 2.0 * math.pi / NFFT * phase
    table = np.concatenate([np.cos(angle), -np.sin(angle)], axis=1)
    return jnp.asarray(table.reshape(QUARTERS, SLICE, 2 * BINS), bf16)


def lag_table():
    phase = (FIRST_BIN + np.arange(BINS))[None, :] * (np.arange(2 * MAX_LAG) - MAX_LAG)[:, None] % NFFT
    angle = 2.0 * math.pi / NFFT * phase
    table = np.concatenate([np.cos(angle), -np.sin(angle)], axis=1)
    return jnp.asarray(jnp.asarray(table, bf16).astype(f32) / math.sqrt(BINS), bf16)


def order_channels(records_t, assignment):
    block = 512

    def kernel(assign_hbm, rec_hbm, out_ref, assign_ref, rec_ref, turn_ref, sems):
        assign_in = pltpu.make_async_copy(assign_hbm, assign_ref, sems.at[0])
        rec_in = pltpu.make_async_copy(rec_hbm, rec_ref, sems.at[1])
        assign_in.start()
        rec_in.start()
        assign_in.wait()
        chan = lax.broadcasted_iota(jnp.int32, (CHANS, block), 0)
        for n in range(CHANS // block):
            at = slice(n * block, (n + 1) * block)
            onehot = (chan == assign_ref[:, at]).astype(f32).astype(bf16)
            if n == 0:
                rec_in.wait()
            turn_ref[n, 0:SLICE, :] = jnp.dot(rec_ref[...], onehot, preferred_element_type=f32)
            out_ref[at, :] = turn_ref[n].T[:, :SLICE].astype(bf16)

    return pl.pallas_call(
        kernel,
        out_shape=jax.ShapeDtypeStruct((CHANS, SLICE), bf16),
        in_specs=[anym, anym],
        out_specs=vmem,
        scratch_shapes=[
            pltpu.VMEM((1, CHANS), jnp.int32),
            pltpu.VMEM((SLICE, CHANS), bf16),
            pltpu.VMEM((CHANS // block, 256, block), f32),
            pltpu.SemaphoreType.DMA((2,)),
        ],
        compiler_params=pltpu.CompilerParams(vmem_limit_bytes=58 * 2**20),
    )(assignment.reshape(1, CHANS), records_t)


def whiten(slices, keep, table):
    def kernel(x_ref, keep_ref, f_ref, out_ref, again_ref, z0, z1, z2, z3, turn_ref, sem):
        zs = [z0, z1, z2, z3]
        spec = None
        for quarter in range(QUARTERS):
            rows = jnp.concatenate([x_ref[QUARTERS * w + quarter] for w in range(WINDOWS)], axis=0)
            part = jnp.dot(rows, f_ref[quarter], preferred_element_type=f32)
            spec = part if spec is None else spec + part
        re, im = spec[:, :BINS], spec[:, BINS:]
        power = re * re + im * im
        water = jnp.mean(power, axis=1, keepdims=True)
        padded = jnp.concatenate([power, jnp.zeros((512, 128), f32)], axis=1)
        total = padded + pltpu.roll(padded, 1, 1)
        total = total + pltpu.roll(total, 2, 1)
        total = total + pltpu.roll(total, 4, 1)
        total = total + pltpu.roll(padded, 8, 1)
        smooth = pltpu.roll(total, 384 - 4, 1)[:, :BINS]
        amp = lax.rsqrt(smooth / 9.0 + 0.1 * water + 1e-6) * keep_ref[...]
        for h in range(4):
            zs[h][...] = spec[:, h * 128 : (h + 1) * 128] * amp[:, (h % 2) * 128 : (h % 2) * 128 + 128]
        low = lax.broadcasted_iota(jnp.int32, (WINDOWS, 128), 1) < 64
        for ri in range(2):
            for pair in range(GROUP // 2):
                rows = []
                for h in range(2):
                    first = zs[2 * ri + h][pl.ds(2 * pair, WINDOWS, stride=GROUP), :]
                    second = zs[2 * ri + h][pl.ds(2 * pair + 1, WINDOWS, stride=GROUP), :]
                    rows.append(jnp.where(low, first, pltpu.roll(second, 64, 1)))
                    rows.append(jnp.where(low, pltpu.roll(first, 64, 1), second))
                turned = jnp.concatenate(rows, axis=0).T
                for j in range(2):
                    turn_ref[pl.ds(ri * GROUP + 2 * pair + j, KGS, stride=2 * GROUP), :] = turned[
                        j * KGS : (j + 1) * KGS
                    ]
        out_ref[...] = turn_ref[...].astype(bf16)
        copy = pltpu.make_async_copy(out_ref, again_ref, sem)
        copy.start()
        copy.wait()

    outs = pl.pallas_call(
        kernel,
        out_shape=[jax.ShapeDtypeStruct((KGS * 2 * GROUP, 128), bf16)] * 2,
        in_specs=[vmem] * 3,
        out_specs=[vmem, anym],
        scratch_shapes=[pltpu.VMEM((512, 128), f32)] * 4
        + [pltpu.VMEM((KGS * 2 * GROUP, 128), f32), pltpu.SemaphoreType.DMA],
        compiler_params=pltpu.CompilerParams(vmem_limit_bytes=40 * 2**20),
    )(slices, keep, table)
    return [out.reshape(KGS, 2, GROUP, 128) for out in outs]


def after(arrays, others):
    count = len(arrays)
    return pl.pallas_call(
        lambda *refs: None,
        out_shape=[jax.ShapeDtypeStruct(a.shape, a.dtype) for a in arrays],
        in_specs=[anym] * (count + len(others)),
        out_specs=[anym] * count,
        input_output_aliases={n: n for n in range(count)},
        cost_estimate=pl.CostEstimate(flops=0, bytes_accessed=0, transcendentals=0),
    )(*arrays, *others)


def pair_chunk(blocks, call, places, second, scale, table, result):
    count = len(blocks)
    rows = count * GROUP

    def kernel(*refs):
        place_ref, scale_ref, tab_ref = refs[:3]
        out_hbm, held, spec_re, spec_im, stage, in_sems, sems = refs[-7:]
        half = KGS // 2

        def copy_in(n, h):
            at = pl.ds(h * half, half)
            return pltpu.make_async_copy(refs[3 + n].at[at], held.at[n, at], in_sems.at[n, h])

        def start(b):
            return pl.multiple_of(place_ref[call * count + b] * GROUP, GROUP)

        def copy_out(b):
            return pltpu.make_async_copy(stage.at[b], out_hbm.at[pl.ds(start(b), GROUP)], sems.at[b])

        for h in range(2):
            for n in range(8 + count):
                copy_in(n, h).start()
        lane = lax.broadcasted_iota(jnp.int32, (rows, 256), 1) % 128 // 32
        columns = [pl.multiple_of(place_ref[4 * count + b] * GROUP, GROUP) for b in range(8)]
        scales = jnp.concatenate([scale_ref[pl.ds(start(b), GROUP), :] for b in range(count)], axis=0)

        @pl.loop(0, 2)
        def _(h):
            for n in range(8 + count):
                copy_in(n, h).wait()

            @pl.loop(0, half, unroll=half)
            def _(i):
                kg = h * half + i
                vr, vi = [jnp.concatenate([held[b, kg, ri] for b in range(8)], axis=0) for ri in range(2)]
                rhs = jnp.concatenate(
                    [jnp.concatenate([vr, vi], axis=1), jnp.concatenate([-vi, vr], axis=1)], axis=0
                )
                lhs = jnp.concatenate(
                    [jnp.concatenate([held[8 + b, kg, ri] for b in range(count)], axis=0) for ri in range(2)],
                    axis=1,
                )
                lhs = jnp.concatenate([jnp.where(lane == ki, lhs, jnp.zeros_like(lhs)) for ki in range(4)], axis=0)
                cross = lax.dot_general(lhs, rhs, (((1,), (1,)), ((), ())), preferred_element_type=f32)
                for ki in range(4):
                    part = cross[ki * rows : (ki + 1) * rows]
                    spec_re[pl.ds(ki * KGS + kg, rows, stride=PITCH), :] = part[:, :128] * scales
                    spec_im[pl.ds(ki * KGS + kg, rows, stride=PITCH), :] = part[:, 128:] * scales

        @pl.loop(0, count // 2)
        def _(couple):
            for i in range(GROUP):
                b = 2 * couple + i // (GROUP // 2)
                row = 2 * (i % (GROUP // 2))
                halves = []
                for ref in (spec_re, spec_im):
                    at = [pl.multiple_of((b * GROUP + row + j) * PITCH, 8) for j in range(2)]
                    halves.append(jnp.concatenate([ref[pl.ds(a, BINS), :].astype(bf16) for a in at], axis=1))
                lagged = lax.dot_general(
                    jnp.concatenate(halves, axis=0),
                    tab_ref[...],
                    (((0,), (1,)), ((), ())),
                    preferred_element_type=f32,
                ).astype(bf16)
                for j in range(2):
                    for c in range(8):
                        at = j * 128 + c * GROUP
                        stage[b, row + j, pl.ds(columns[c], GROUP), :] = lagged[at : at + GROUP]
            for b in range(2):
                copy_out(2 * couple + b).start()

        for b in range(count):
            copy_out(b).wait()

    ins = [places, scale, table, *second, *blocks]
    specs = [smem, vmem, vmem] + [anym] * (8 + count)
    aliases = {}
    if result is not None:
        aliases = {len(ins): 0}
        ins.append(result)
        specs.append(anym)
    return pl.pallas_call(
        kernel,
        out_shape=jax.ShapeDtypeStruct((256, 128, 2 * MAX_LAG), bf16),
        in_specs=specs,
        out_specs=anym,
        scratch_shapes=[
            pltpu.VMEM((8 + count, KGS, 2, GROUP, 128), bf16),
            pltpu.VMEM((rows * PITCH, 128), f32),
            pltpu.VMEM((rows * PITCH, 128), f32),
            pltpu.VMEM((count, GROUP, 128, 2 * MAX_LAG), bf16),
            pltpu.SemaphoreType.DMA((8 + count, 2)),
            pltpu.SemaphoreType.DMA((count,)),
        ],
        input_output_aliases=aliases,
        compiler_params=pltpu.CompilerParams(vmem_limit_bytes=58 * 2**20),
        cost_estimate=pl.CostEstimate(flops=8 * 10**9, bytes_accessed=10 * 2**20, transcendentals=0),
    )(*ins)


def col_perm(dz, dx, dcore):
    def to(i):
        z, x, core = i // 8, i // 2 % 4, i % 2
        return ((z ^ dz) * 4 + (x + dx) % 4) * 2 + (core ^ dcore)

    return [(i, to(i)) for i in range(16)]


def row_perm(dz, dy):
    return [(i, (i // 4 ^ dz) * 4 + (i % 4 + dy) % 4) for i in range(8)]


def per_device(records, assignment, channel_flags):
    row = lax.axis_index("row")
    col = lax.axis_index("col")
    layout = assignment.reshape(8, 16, GROUP)
    z_lo, y = row // 4, row % 4
    z_hi, x, core = col // 8, col // 2 % 4, col % 2
    steps = (0, -1, 1, 2)
    second_places = [(z_lo ^ dz) * 4 + (y + d) % 4 for dz in range(2) for d in steps]
    row_chans = lax.dynamic_index_in_dim(layout, row, 0, keepdims=False).reshape(-1)
    col_layout = lax.dynamic_index_in_dim(layout, col, 1, keepdims=False)
    col_chans = jnp.take(col_layout, jnp.stack(second_places), axis=0, mode="clip").reshape(-1)
    own_row = lax.dynamic_index_in_dim(layout, row, 0, keepdims=False)
    own_chans = lax.dynamic_index_in_dim(own_row, col, 0, keepdims=False)

    ordered = order_channels(records.T, assignment)
    slices = lax.all_to_all(
        ordered.reshape(128, GROUP, SLICE), ("row", "col"), split_axis=0, concat_axis=0, tiled=True
    )

    flags = channel_flags.astype(f32)
    row_flags = jnp.take(flags, row_chans, axis=1, mode="clip")
    col_flags = jnp.take(flags, col_chans, axis=1, mode="clip")
    keep = jnp.take(flags, own_chans, axis=1, mode="clip").reshape(WINDOWS * GROUP, 1)
    shared = jnp.dot(jnp.transpose(row_flags), col_flags, precision=lax.Precision.HIGHEST)
    scale = lax.rsqrt(jnp.maximum(shared, 1.0))

    first_places = [
        ((z_hi ^ dz) * 4 + (x + d) % 4) * 2 + (core ^ dc) for dz in range(2) for dc in range(2) for d in steps
    ]
    places = jnp.stack(first_places + second_places).astype(jnp.int32)
    slices, keep, scale, places = lax.optimization_barrier((slices, keep, scale, places))
    own, again = whiten(slices, keep, forward_table())

    y_up, y_down = row_perm(0, 1), row_perm(0, -1)
    x_up, x_down, flip = col_perm(0, 1, 0), col_perm(0, -1, 0), col_perm(0, 0, 1)

    def along_row(block, perm, name):
        with jax.named_scope(name):
            return lax.ppermute(block, "row", perm)

    def along_col(block, perm, name):
        with jax.named_scope(name):
            return lax.ppermute(block, "col", perm)

    zl = along_row(own, row_perm(1, 0), "zl")
    y_below, y_above = along_row(own, y_up, "y_below"), along_row(own, y_down, "y_above")
    x_below, x_above = along_col(own, x_up, "x_below"), along_col(own, x_down, "x_above")

    (again,) = after([again], [zl, y_below, y_above])
    zl_below, zl_above = along_row(zl, y_up, "zl_below"), along_row(zl, y_down, "zl_above")
    zh = along_col(again, col_perm(1, 0, 0), "zh")
    x_far = along_col(x_below, x_up, "x_far")
    x_far_other = along_col(x_above, col_perm(0, -1, 1), "x_far_other")

    (y_below,) = after([y_below], [zl_below])
    y_far, zl_far = along_row(y_below, y_up, "y_far"), along_row(zl_above, y_down, "zl_far")
    zh_below, zh_above = along_col(zh, x_up, "zh_below"), along_col(zh, x_down, "zh_above")
    zh_far = along_col(x_far, col_perm(1, 0, 0), "zh_far")
    again, x_below, x_above = after([again, x_below, x_above], [zl_below, zl_above, zh, x_far, x_far_other])
    swaps = [along_col(block, flip, "core_swap") for block in (again, x_below, x_above)]

    second = [own, y_below, y_above, y_far, zl, zl_below, zl_above, zl_far]
    table = lag_table()
    result = pair_chunk([own, x_below, x_above, x_far], 0, places, second, scale, table, None)
    result = pair_chunk([*swaps, x_far_other], 1, places, second, scale, table, result)
    blocks = after([zh, zh_below, zh_above, zh_far], [result])
    swaps = [along_col(block, flip, "core_swap") for block in blocks]
    result = pair_chunk(blocks, 2, places, second, scale, table, result)
    result = pair_chunk(swaps, 3, places, second, scale, table, result)
    return result


def solution(mesh):
    placed = (P(None, ("row", "col")), P(), P())
    return jax.shard_map(
        per_device, mesh=mesh, in_specs=placed, out_specs=P("row", "col", None), check_vma=False
    )
```

```python
import math

import jax
import jax.numpy as jnp
import numpy as np
from jax import lax
from jax.experimental import pallas as pl
from jax.experimental.pallas import tpu as pltpu
from jax.sharding import PartitionSpec as P

SAMPLES = 600
NFFT = 1024
FIRST_BIN = 10
BINS = 256
MAX_LAG = 128
WINDOWS = 32
CHANS = 2048
GROUP = 16
SLICE = 150
QUARTERS = 4
KGS = 64
PITCH = 264

f32 = jnp.float32
bf16 = jnp.bfloat16
vmem = pl.BlockSpec(memory_space=pltpu.VMEM)
smem = pl.BlockSpec(memory_space=pltpu.SMEM)
anym = pl.BlockSpec(memory_space=pl.ANY)


def forward_table():
    phase = (FIRST_BIN + np.arange(BINS))[None, :] * np.arange(SAMPLES)[:, None] % NFFT
    angle = 2.0 * math.pi / NFFT * phase
    table = np.concatenate([np.cos(angle), -np.sin(angle)], axis=1)
    return jnp.asarray(table.reshape(QUARTERS, SLICE, 2 * BINS), bf16)


def lag_table():
    phase = (FIRST_BIN + np.arange(BINS))[None, :] * (np.arange(2 * MAX_LAG) - MAX_LAG)[:, None] % NFFT
    angle = 2.0 * math.pi / NFFT * phase
    table = np.concatenate([np.cos(angle), -np.sin(angle)], axis=1)
    return jnp.asarray(jnp.asarray(table, bf16).astype(f32) / math.sqrt(BINS), bf16)


def order_channels(records_t, assignment):
    block = 512

    def kernel(assign_hbm, rec_hbm, out_ref, assign_ref, rec_ref, turn_ref, sems):
        assign_in = pltpu.make_async_copy(assign_hbm, assign_ref, sems.at[0])
        rec_in = pltpu.make_async_copy(rec_hbm, rec_ref, sems.at[1])
        assign_in.start()
        rec_in.start()
        assign_in.wait()
        chan = lax.broadcasted_iota(jnp.int32, (CHANS, block), 0)
        for n in range(CHANS // block):
            at = slice(n * block, (n + 1) * block)
            onehot = (chan == assign_ref[:, at]).astype(f32).astype(bf16)
            if n == 0:
                rec_in.wait()
            turn_ref[n, 0:SLICE, :] = jnp.dot(rec_ref[...], onehot, preferred_element_type=f32)
            out_ref[at, :] = turn_ref[n].T[:, :SLICE].astype(bf16)

    return pl.pallas_call(
        kernel,
        out_shape=jax.ShapeDtypeStruct((CHANS, SLICE), bf16),
        in_specs=[anym, anym],
        out_specs=vmem,
        scratch_shapes=[
            pltpu.VMEM((1, CHANS), jnp.int32),
            pltpu.VMEM((SLICE, CHANS), bf16),
            pltpu.VMEM((CHANS // block, 256, block), f32),
            pltpu.SemaphoreType.DMA((2,)),
        ],
        compiler_params=pltpu.CompilerParams(vmem_limit_bytes=58 * 2**20),
    )(assignment.reshape(1, CHANS), records_t)


def whiten(slices, keep, table):
    def kernel(x_ref, keep_ref, f_ref, out_ref, again_ref, z0, z1, z2, z3, turn_ref, sem):
        zs = [z0, z1, z2, z3]
        spec = None
        for quarter in range(QUARTERS):
            rows = jnp.concatenate([x_ref[QUARTERS * w + quarter] for w in range(WINDOWS)], axis=0)
            part = jnp.dot(rows, f_ref[quarter], preferred_element_type=f32)
            spec = part if spec is None else spec + part
        re, im = spec[:, :BINS], spec[:, BINS:]
        power = re * re + im * im
        water = jnp.mean(power, axis=1, keepdims=True)
        padded = jnp.concatenate([power, jnp.zeros((512, 128), f32)], axis=1)
        total = padded + pltpu.roll(padded, 1, 1)
        total = total + pltpu.roll(total, 2, 1)
        total = total + pltpu.roll(total, 4, 1)
        total = total + pltpu.roll(padded, 8, 1)
        smooth = pltpu.roll(total, 384 - 4, 1)[:, :BINS]
        amp = lax.rsqrt(smooth / 9.0 + 0.1 * water + 1e-6) * keep_ref[...]
        for h in range(4):
            zs[h][...] = spec[:, h * 128 : (h + 1) * 128] * amp[:, (h % 2) * 128 : (h % 2) * 128 + 128]
        low = lax.broadcasted_iota(jnp.int32, (WINDOWS, 128), 1) < 64
        for ri in range(2):
            for pair in range(GROUP // 2):
                rows = []
                for h in range(2):
                    first = zs[2 * ri + h][pl.ds(2 * pair, WINDOWS, stride=GROUP), :]
                    second = zs[2 * ri + h][pl.ds(2 * pair + 1, WINDOWS, stride=GROUP), :]
                    rows.append(jnp.where(low, first, pltpu.roll(second, 64, 1)))
                    rows.append(jnp.where(low, pltpu.roll(first, 64, 1), second))
                turned = jnp.concatenate(rows, axis=0).T
                for j in range(2):
                    turn_ref[pl.ds(ri * GROUP + 2 * pair + j, KGS, stride=2 * GROUP), :] = turned[
                        j * KGS : (j + 1) * KGS
                    ]
        out_ref[...] = turn_ref[...].astype(bf16)
        copy = pltpu.make_async_copy(out_ref, again_ref, sem)
        copy.start()
        copy.wait()

    outs = pl.pallas_call(
        kernel,
        out_shape=[jax.ShapeDtypeStruct((KGS * 2 * GROUP, 128), bf16)] * 2,
        in_specs=[vmem] * 3,
        out_specs=[vmem, anym],
        scratch_shapes=[pltpu.VMEM((512, 128), f32)] * 4
        + [pltpu.VMEM((KGS * 2 * GROUP, 128), f32), pltpu.SemaphoreType.DMA],
        compiler_params=pltpu.CompilerParams(vmem_limit_bytes=40 * 2**20),
    )(slices, keep, table)
    return [out.reshape(KGS, 2, GROUP, 128) for out in outs]


def after(arrays, others):
    count = len(arrays)
    return pl.pallas_call(
        lambda *refs: None,
        out_shape=[jax.ShapeDtypeStruct(a.shape, a.dtype) for a in arrays],
        in_specs=[anym] * (count + len(others)),
        out_specs=[anym] * count,
        input_output_aliases={n: n for n in range(count)},
        cost_estimate=pl.CostEstimate(flops=0, bytes_accessed=0, transcendentals=0),
    )(*arrays, *others)


def pair_chunk(blocks, places, second, scale, table, result):
    count = len(blocks)
    group = 4
    rows = group * GROUP

    def kernel(*refs):
        place_ref, scale_ref, tab_ref = refs[:3]
        out_hbm, held, spec_re, spec_im, stage, in_sems, sems = refs[-7:]
        half = KGS // 2

        def copy_in(n, h):
            at = pl.ds(h * half, half)
            return pltpu.make_async_copy(refs[3 + n].at[at], held.at[n, at], in_sems.at[n, h])

        def copy_out(b):
            at = pl.multiple_of(place_ref[b] * GROUP, GROUP)
            return pltpu.make_async_copy(stage.at[b], out_hbm.at[pl.ds(at, GROUP)], sems.at[b])

        for h in range(2):
            for n in range(8 + group):
                copy_in(n, h).start()
        for n in range(8 + group, 8 + count):
            for h in range(2):
                copy_in(n, h).start()
        lane = lax.broadcasted_iota(jnp.int32, (rows, 256), 1) % 128 // 32
        columns = [pl.multiple_of(place_ref[count + b] * GROUP, GROUP) for b in range(8)]

        @pl.loop(0, count // group)
        def _(turn):
            base = turn * group
            starts = [pl.multiple_of(place_ref[base + b] * GROUP, GROUP) for b in range(group)]
            scales = jnp.concatenate([scale_ref[pl.ds(at, GROUP), :] for at in starts], axis=0)

            @pl.loop(0, 2)
            def _(h):
                @pl.when(turn == 0)
                def _():
                    for n in range(8 + group):
                        copy_in(n, h).wait()

                @pl.when(turn > 0)
                def _():
                    for n in range(8 + group, 8 + count):
                        copy_in(n, h).wait()

                @pl.loop(0, half, unroll=half)
                def _(i):
                    kg = h * half + i
                    vr, vi = [jnp.concatenate([held[b, kg, ri] for b in range(8)], axis=0) for ri in range(2)]
                    rhs = jnp.concatenate(
                        [jnp.concatenate([vr, vi], axis=1), jnp.concatenate([-vi, vr], axis=1)], axis=0
                    )
                    lhs = jnp.concatenate(
                        [
                            jnp.concatenate([held[8 + base + b, kg, ri] for b in range(group)], axis=0)
                            for ri in range(2)
                        ],
                        axis=1,
                    )
                    lhs = jnp.concatenate(
                        [jnp.where(lane == ki, lhs, jnp.zeros_like(lhs)) for ki in range(4)], axis=0
                    )
                    cross = lax.dot_general(lhs, rhs, (((1,), (1,)), ((), ())), preferred_element_type=f32)
                    for ki in range(4):
                        part = cross[ki * rows : (ki + 1) * rows]
                        spec_re[pl.ds(ki * KGS + kg, rows, stride=PITCH), :] = part[:, :128] * scales
                        spec_im[pl.ds(ki * KGS + kg, rows, stride=PITCH), :] = part[:, 128:] * scales

            @pl.loop(0, group // 2)
            def _(couple):
                for i in range(GROUP):
                    b = 2 * couple + i // (GROUP // 2)
                    row = 2 * (i % (GROUP // 2))
                    halves = []
                    for ref in (spec_re, spec_im):
                        at = [pl.multiple_of((b * GROUP + row + j) * PITCH, 8) for j in range(2)]
                        halves.append(
                            jnp.concatenate([ref[pl.ds(a, BINS), :].astype(bf16) for a in at], axis=1)
                        )
                    lagged = lax.dot_general(
                        jnp.concatenate(halves, axis=0),
                        tab_ref[...],
                        (((0,), (1,)), ((), ())),
                        preferred_element_type=f32,
                    ).astype(bf16)
                    for j in range(2):
                        for c in range(8):
                            at = j * 128 + c * GROUP
                            stage[base + b, row + j, pl.ds(columns[c], GROUP), :] = lagged[at : at + GROUP]
                for b in range(2):
                    copy_out(base + 2 * couple + b).start()

        for b in range(count):
            copy_out(b).wait()

    ins = [places, scale, table, *second, *blocks]
    specs = [smem, vmem, vmem] + [anym] * (8 + count)
    aliases = {}
    if result is not None:
        aliases = {len(ins): 0}
        ins.append(result)
        specs.append(anym)
    return pl.pallas_call(
        kernel,
        out_shape=jax.ShapeDtypeStruct((256, 128, 2 * MAX_LAG), bf16),
        in_specs=specs,
        out_specs=anym,
        scratch_shapes=[
            pltpu.VMEM((8 + count, KGS, 2, GROUP, 128), bf16),
            pltpu.VMEM((rows * PITCH, 128), f32),
            pltpu.VMEM((rows * PITCH, 128), f32),
            pltpu.VMEM((count, GROUP, 128, 2 * MAX_LAG), bf16),
            pltpu.SemaphoreType.DMA((8 + count, 2)),
            pltpu.SemaphoreType.DMA((count,)),
        ],
        input_output_aliases=aliases,
        compiler_params=pltpu.CompilerParams(vmem_limit_bytes=58 * 2**20),
        cost_estimate=pl.CostEstimate(flops=15 * 10**9, bytes_accessed=10 * 2**20, transcendentals=0),
    )(*ins)


def col_perm(dz, dx, dcore):
    def to(i):
        z, x, core = i // 8, i // 2 % 4, i % 2
        return ((z ^ dz) * 4 + (x + dx) % 4) * 2 + (core ^ dcore)

    return [(i, to(i)) for i in range(16)]


def row_perm(dz, dy):
    return [(i, (i // 4 ^ dz) * 4 + (i % 4 + dy) % 4) for i in range(8)]


def per_device(records, assignment, channel_flags):
    row = lax.axis_index("row")
    col = lax.axis_index("col")
    layout = assignment.reshape(8, 16, GROUP)
    z_lo, y = row // 4, row % 4
    z_hi, x, core = col // 8, col // 2 % 4, col % 2
    steps = (0, -1, 1, 2)
    second_places = [(z_lo ^ dz) * 4 + (y + d) % 4 for dz in range(2) for d in steps]
    row_chans = lax.dynamic_index_in_dim(layout, row, 0, keepdims=False).reshape(-1)
    col_layout = lax.dynamic_index_in_dim(layout, col, 1, keepdims=False)
    col_chans = jnp.take(col_layout, jnp.stack(second_places), axis=0, mode="clip").reshape(-1)
    own_row = lax.dynamic_index_in_dim(layout, row, 0, keepdims=False)
    own_chans = lax.dynamic_index_in_dim(own_row, col, 0, keepdims=False)

    ordered = order_channels(records.T, assignment)
    slices = lax.all_to_all(
        ordered.reshape(128, GROUP, SLICE), ("row", "col"), split_axis=0, concat_axis=0, tiled=True
    )

    flags = channel_flags.astype(f32)
    row_flags = jnp.take(flags, row_chans, axis=1, mode="clip")
    col_flags = jnp.take(flags, col_chans, axis=1, mode="clip")
    keep = jnp.take(flags, own_chans, axis=1, mode="clip").reshape(WINDOWS * GROUP, 1)
    shared = jnp.dot(jnp.transpose(row_flags), col_flags, precision=lax.Precision.HIGHEST)
    scale = lax.rsqrt(jnp.maximum(shared, 1.0))

    places = [
        jnp.stack(
            [((z_hi ^ dz) * 4 + (x + d) % 4) * 2 + (core ^ dc) for dc in range(2) for d in steps] + second_places
        ).astype(jnp.int32)
        for dz in range(2)
    ]
    slices, keep, scale, places = lax.optimization_barrier((slices, keep, scale, places))
    own, again = whiten(slices, keep, forward_table())

    y_up, y_down = row_perm(0, 1), row_perm(0, -1)
    x_up, x_down, flip = col_perm(0, 1, 0), col_perm(0, -1, 0), col_perm(0, 0, 1)

    def along_row(block, perm, name):
        with jax.named_scope(name):
            return lax.ppermute(block, "row", perm)

    def along_col(block, perm, name):
        with jax.named_scope(name):
            return lax.ppermute(block, "col", perm)

    zl = along_row(own, row_perm(1, 0), "zl")
    y_below, y_above = along_row(own, y_up, "y_below"), along_row(own, y_down, "y_above")
    x_below, x_above = along_col(own, x_up, "x_below"), along_col(own, x_down, "x_above")

    (again,) = after([again], [zl, y_below, y_above])
    zl_below, zl_above = along_row(zl, y_up, "zl_below"), along_row(zl, y_down, "zl_above")
    zh = along_col(again, col_perm(1, 0, 0), "zh")
    x_far = along_col(x_below, x_up, "x_far")
    x_far_other = along_col(x_above, col_perm(0, -1, 1), "x_far_other")

    (y_below,) = after([y_below], [zl_below])
    y_far, zl_far = along_row(y_below, y_up, "y_far"), along_row(zl_above, y_down, "zl_far")
    zh_below, zh_above = along_col(zh, x_up, "zh_below"), along_col(zh, x_down, "zh_above")
    zh_far = along_col(x_far, col_perm(1, 0, 0), "zh_far")
    again, x_below, x_above = after([again, x_below, x_above], [zl_below, zl_above, zh, x_far, x_far_other])
    swaps = [along_col(block, flip, "core_swap") for block in (again, x_below, x_above)]

    second = [own, y_below, y_above, y_far, zl, zl_below, zl_above, zl_far]
    table = lag_table()
    blocks = [own, x_below, x_above, x_far, *swaps, x_far_other]
    result = pair_chunk(blocks, places[0], second, scale, table, None)
    blocks = after([zh, zh_below, zh_above, zh_far], [result])
    blocks = [*blocks, *(along_col(block, flip, "core_swap") for block in blocks)]
    result = pair_chunk(blocks, places[1], second, scale, table, result)
    return result


def solution(mesh):
    placed = (P(None, ("row", "col")), P(), P())
    return jax.shard_map(
        per_device, mesh=mesh, in_specs=placed, out_specs=P("row", "col", None), check_vma=False
    )
```

```python
import math

import jax
import jax.numpy as jnp
import numpy as np
from jax import lax
from jax.experimental import pallas as pl
from jax.experimental.pallas import tpu as pltpu
from jax.sharding import PartitionSpec as P

SAMPLES = 600
NFFT = 1024
FIRST_BIN = 10
BINS = 256
MAX_LAG = 128
WINDOWS = 32
CHANS = 2048
GROUP = 16
SLICE = 150
QUARTERS = 4
KGS = 64
PITCH = 264

f32 = jnp.float32
bf16 = jnp.bfloat16
vmem = pl.BlockSpec(memory_space=pltpu.VMEM)
smem = pl.BlockSpec(memory_space=pltpu.SMEM)
anym = pl.BlockSpec(memory_space=pl.ANY)


def forward_table():
    phase = (FIRST_BIN + np.arange(BINS))[None, :] * np.arange(SAMPLES)[:, None] % NFFT
    angle = 2.0 * math.pi / NFFT * phase
    table = np.concatenate([np.cos(angle), -np.sin(angle)], axis=1)
    return jnp.asarray(table.reshape(QUARTERS, SLICE, 2 * BINS), bf16)


def lag_table():
    phase = (FIRST_BIN + np.arange(BINS))[None, :] * (np.arange(2 * MAX_LAG) - MAX_LAG)[:, None] % NFFT
    angle = 2.0 * math.pi / NFFT * phase
    table = np.concatenate([np.cos(angle), -np.sin(angle)], axis=1)
    return jnp.asarray(jnp.asarray(table, bf16).astype(f32) / math.sqrt(BINS), bf16)


def order_channels(records_t, assignment):
    block = 512

    def kernel(assign_hbm, rec_hbm, out_ref, assign_ref, rec_ref, turn_ref, sems):
        assign_in = pltpu.make_async_copy(assign_hbm, assign_ref, sems.at[0])
        rec_in = pltpu.make_async_copy(rec_hbm, rec_ref, sems.at[1])
        assign_in.start()
        rec_in.start()
        assign_in.wait()
        chan = lax.broadcasted_iota(jnp.int32, (CHANS, block), 0)
        for n in range(CHANS // block):
            at = slice(n * block, (n + 1) * block)
            onehot = (chan == assign_ref[:, at]).astype(f32).astype(bf16)
            if n == 0:
                rec_in.wait()
            turn_ref[n, 0:SLICE, :] = jnp.dot(rec_ref[...], onehot, preferred_element_type=f32)
            out_ref[at, :] = turn_ref[n].T[:, :SLICE].astype(bf16)

    return pl.pallas_call(
        kernel,
        out_shape=jax.ShapeDtypeStruct((CHANS, SLICE), bf16),
        in_specs=[anym, anym],
        out_specs=vmem,
        scratch_shapes=[
            pltpu.VMEM((1, CHANS), jnp.int32),
            pltpu.VMEM((SLICE, CHANS), bf16),
            pltpu.VMEM((CHANS // block, 256, block), f32),
            pltpu.SemaphoreType.DMA((2,)),
        ],
        compiler_params=pltpu.CompilerParams(vmem_limit_bytes=58 * 2**20),
    )(assignment.reshape(1, CHANS), records_t)


def whiten(slices, keep, table):
    def kernel(x_ref, keep_ref, f_ref, out_ref, again_ref, z0, z1, z2, z3, turn_ref, sem):
        zs = [z0, z1, z2, z3]
        spec = None
        for quarter in range(QUARTERS):
            rows = jnp.concatenate([x_ref[QUARTERS * w + quarter] for w in range(WINDOWS)], axis=0)
            part = jnp.dot(rows, f_ref[quarter], preferred_element_type=f32)
            spec = part if spec is None else spec + part
        re, im = spec[:, :BINS], spec[:, BINS:]
        power = re * re + im * im
        water = jnp.mean(power, axis=1, keepdims=True)
        padded = jnp.concatenate([power, jnp.zeros((512, 128), f32)], axis=1)
        total = padded + pltpu.roll(padded, 1, 1)
        total = total + pltpu.roll(total, 2, 1)
        total = total + pltpu.roll(total, 4, 1)
        total = total + pltpu.roll(padded, 8, 1)
        smooth = pltpu.roll(total, 384 - 4, 1)[:, :BINS]
        amp = lax.rsqrt(smooth / 9.0 + 0.1 * water + 1e-6) * keep_ref[...]
        for h in range(4):
            zs[h][...] = spec[:, h * 128 : (h + 1) * 128] * amp[:, (h % 2) * 128 : (h % 2) * 128 + 128]
        low = lax.broadcasted_iota(jnp.int32, (WINDOWS, 128), 1) < 64
        for ri in range(2):
            for pair in range(GROUP // 2):
                rows = []
                for h in range(2):
                    first = zs[2 * ri + h][pl.ds(2 * pair, WINDOWS, stride=GROUP), :]
                    second = zs[2 * ri + h][pl.ds(2 * pair + 1, WINDOWS, stride=GROUP), :]
                    rows.append(jnp.where(low, first, pltpu.roll(second, 64, 1)))
                    rows.append(jnp.where(low, pltpu.roll(first, 64, 1), second))
                turned = jnp.concatenate(rows, axis=0).T
                for j in range(2):
                    turn_ref[pl.ds(ri * GROUP + 2 * pair + j, KGS, stride=2 * GROUP), :] = turned[
                        j * KGS : (j + 1) * KGS
                    ]
        out_ref[...] = turn_ref[...].astype(bf16)
        copy = pltpu.make_async_copy(out_ref, again_ref, sem)
        copy.start()
        copy.wait()

    outs = pl.pallas_call(
        kernel,
        out_shape=[jax.ShapeDtypeStruct((KGS * 2 * GROUP, 128), bf16)] * 2,
        in_specs=[vmem] * 3,
        out_specs=[vmem, anym],
        scratch_shapes=[pltpu.VMEM((512, 128), f32)] * 4
        + [pltpu.VMEM((KGS * 2 * GROUP, 128), f32), pltpu.SemaphoreType.DMA],
        compiler_params=pltpu.CompilerParams(vmem_limit_bytes=40 * 2**20),
    )(slices, keep, table)
    return [out.reshape(KGS, 2, GROUP, 128) for out in outs]


def bring_in(table):
    def kernel(in_ref, out_ref):
        out_ref[...] = in_ref[...]

    return pl.pallas_call(
        kernel,
        out_shape=jax.ShapeDtypeStruct(table.shape, table.dtype),
        in_specs=[vmem],
        out_specs=vmem,
        compiler_params=pltpu.CompilerParams(vmem_limit_bytes=20 * 2**20),
    )(table)


def after(arrays, others):
    count = len(arrays)
    return pl.pallas_call(
        lambda *refs: None,
        out_shape=[jax.ShapeDtypeStruct(a.shape, a.dtype) for a in arrays],
        in_specs=[anym] * (count + len(others)),
        out_specs=[anym] * count,
        input_output_aliases={n: n for n in range(count)},
        cost_estimate=pl.CostEstimate(flops=0, bytes_accessed=0, transcendentals=0),
    )(*arrays, *others)


def pair_chunk(blocks, places, second, scale, table, result):
    count = len(blocks)
    group = 4
    rows = group * GROUP

    def kernel(*refs):
        place_ref, scale_ref, tab_ref = refs[:3]
        out_hbm, held, spec_re, spec_im, stage, in_sems, sems = refs[-7:]
        half = KGS // 2

        def copy_in(n, h):
            at = pl.ds(h * half, half)
            return pltpu.make_async_copy(refs[3 + n].at[at], held.at[n, at], in_sems.at[n, h])

        def copy_out(b):
            at = pl.multiple_of(place_ref[b] * GROUP, GROUP)
            return pltpu.make_async_copy(stage.at[b], out_hbm.at[pl.ds(at, GROUP)], sems.at[b])

        for h in range(2):
            for n in range(8 + group):
                copy_in(n, h).start()
        for n in range(8 + group, 8 + count):
            for h in range(2):
                copy_in(n, h).start()
        lane = lax.broadcasted_iota(jnp.int32, (rows, 256), 1) % 128 // 32
        columns = [pl.multiple_of(place_ref[count + b] * GROUP, GROUP) for b in range(8)]

        @pl.loop(0, count // group)
        def _(turn):
            base = turn * group
            starts = [pl.multiple_of(place_ref[base + b] * GROUP, GROUP) for b in range(group)]
            scales = jnp.concatenate([scale_ref[pl.ds(at, GROUP), :] for at in starts], axis=0)

            @pl.loop(0, 2)
            def _(h):
                @pl.when(turn == 0)
                def _():
                    for n in range(8 + group):
                        copy_in(n, h).wait()

                @pl.when(turn > 0)
                def _():
                    for n in range(8 + group, 8 + count):
                        copy_in(n, h).wait()

                @pl.loop(0, half, unroll=half)
                def _(i):
                    kg = h * half + i
                    vr, vi = [jnp.concatenate([held[b, kg, ri] for b in range(8)], axis=0) for ri in range(2)]
                    rhs = jnp.concatenate(
                        [jnp.concatenate([vr, vi], axis=1), jnp.concatenate([-vi, vr], axis=1)], axis=0
                    )
                    lhs = jnp.concatenate(
                        [
                            jnp.concatenate([held[8 + base + b, kg, ri] for b in range(group)], axis=0)
                            for ri in range(2)
                        ],
                        axis=1,
                    )
                    lhs = jnp.concatenate(
                        [jnp.where(lane == ki, lhs, jnp.zeros_like(lhs)) for ki in range(4)], axis=0
                    )
                    cross = lax.dot_general(lhs, rhs, (((1,), (1,)), ((), ())), preferred_element_type=f32)
                    for ki in range(4):
                        part = cross[ki * rows : (ki + 1) * rows]
                        spec_re[pl.ds(ki * KGS + kg, rows, stride=PITCH), :] = part[:, :128] * scales
                        spec_im[pl.ds(ki * KGS + kg, rows, stride=PITCH), :] = part[:, 128:] * scales

            @pl.loop(0, group // 2)
            def _(couple):
                for i in range(GROUP):
                    b = 2 * couple + i // (GROUP // 2)
                    row = 2 * (i % (GROUP // 2))
                    halves = []
                    for ref in (spec_re, spec_im):
                        at = [pl.multiple_of((b * GROUP + row + j) * PITCH, 8) for j in range(2)]
                        halves.append(
                            jnp.concatenate([ref[pl.ds(a, BINS), :].astype(bf16) for a in at], axis=1)
                        )
                    lagged = lax.dot_general(
                        jnp.concatenate(halves, axis=0),
                        tab_ref[...],
                        (((0,), (1,)), ((), ())),
                        preferred_element_type=f32,
                    ).astype(bf16)
                    for j in range(2):
                        for c in range(8):
                            at = j * 128 + c * GROUP
                            stage[base + b, row + j, pl.ds(columns[c], GROUP), :] = lagged[at : at + GROUP]
                for b in range(2):
                    copy_out(base + 2 * couple + b).start()

        for b in range(count):
            copy_out(b).wait()

    ins = [places, scale, table, *second, *blocks]
    specs = [smem, vmem, vmem] + [anym] * (8 + count)
    aliases = {}
    if result is not None:
        aliases = {len(ins): 0}
        ins.append(result)
        specs.append(anym)
    return pl.pallas_call(
        kernel,
        out_shape=jax.ShapeDtypeStruct((256, 128, 2 * MAX_LAG), bf16),
        in_specs=specs,
        out_specs=anym,
        scratch_shapes=[
            pltpu.VMEM((8 + count, KGS, 2, GROUP, 128), bf16),
            pltpu.VMEM((rows * PITCH, 128), f32),
            pltpu.VMEM((rows * PITCH, 128), f32),
            pltpu.VMEM((count, GROUP, 128, 2 * MAX_LAG), bf16),
            pltpu.SemaphoreType.DMA((8 + count, 2)),
            pltpu.SemaphoreType.DMA((count,)),
        ],
        input_output_aliases=aliases,
        compiler_params=pltpu.CompilerParams(vmem_limit_bytes=58 * 2**20),
        cost_estimate=pl.CostEstimate(flops=15 * 10**9, bytes_accessed=10 * 2**20, transcendentals=0),
    )(*ins)


def col_perm(dz, dx, dcore):
    def to(i):
        z, x, core = i // 8, i // 2 % 4, i % 2
        return ((z ^ dz) * 4 + (x + dx) % 4) * 2 + (core ^ dcore)

    return [(i, to(i)) for i in range(16)]


def row_perm(dz, dy):
    return [(i, (i // 4 ^ dz) * 4 + (i % 4 + dy) % 4) for i in range(8)]


def per_device(records, assignment, channel_flags):
    row = lax.axis_index("row")
    col = lax.axis_index("col")
    layout = assignment.reshape(8, 16, GROUP)
    z_lo, y = row // 4, row % 4
    z_hi, x, core = col // 8, col // 2 % 4, col % 2
    steps = (0, -1, 1, 2)
    second_places = [(z_lo ^ dz) * 4 + (y + d) % 4 for dz in range(2) for d in steps]
    row_chans = lax.dynamic_index_in_dim(layout, row, 0, keepdims=False).reshape(-1)
    col_layout = lax.dynamic_index_in_dim(layout, col, 1, keepdims=False)
    col_chans = jnp.take(col_layout, jnp.stack(second_places), axis=0, mode="clip").reshape(-1)
    own_row = lax.dynamic_index_in_dim(layout, row, 0, keepdims=False)
    own_chans = lax.dynamic_index_in_dim(own_row, col, 0, keepdims=False)

    ordered = order_channels(records.T, assignment)
    slices = lax.all_to_all(
        ordered.reshape(128, GROUP, SLICE), ("row", "col"), split_axis=0, concat_axis=0, tiled=True
    )

    flags = channel_flags.astype(f32)
    row_flags = jnp.take(flags, row_chans, axis=1, mode="clip")
    col_flags = jnp.take(flags, col_chans, axis=1, mode="clip")
    keep = jnp.take(flags, own_chans, axis=1, mode="clip").reshape(WINDOWS * GROUP, 1)
    shared = jnp.dot(jnp.transpose(row_flags), col_flags, precision=lax.Precision.HIGHEST)
    scale = lax.rsqrt(jnp.maximum(shared, 1.0))

    places = [
        jnp.stack(
            [((z_hi ^ dz) * 4 + (x + d) % 4) * 2 + (core ^ dc) for dc in range(2) for d in steps] + second_places
        ).astype(jnp.int32)
        for dz in range(2)
    ]
    forward = bring_in(forward_table())
    slices, keep, scale, places, forward = lax.optimization_barrier((slices, keep, scale, places, forward))
    own, again = whiten(slices, keep, forward)

    y_up, y_down = row_perm(0, 1), row_perm(0, -1)
    x_up, x_down, flip = col_perm(0, 1, 0), col_perm(0, -1, 0), col_perm(0, 0, 1)

    def along_row(block, perm, name):
        with jax.named_scope(name):
            return lax.ppermute(block, "row", perm)

    def along_col(block, perm, name):
        with jax.named_scope(name):
            return lax.ppermute(block, "col", perm)

    zl = along_row(own, row_perm(1, 0), "zl")
    y_below, y_above = along_row(own, y_up, "y_below"), along_row(own, y_down, "y_above")
    x_below, x_above = along_col(own, x_up, "x_below"), along_col(own, x_down, "x_above")

    (again,) = after([again], [zl, y_below, y_above])
    zl_below, zl_above = along_row(zl, y_up, "zl_below"), along_row(zl, y_down, "zl_above")
    zh = along_col(again, col_perm(1, 0, 0), "zh")
    x_far = along_col(x_below, x_up, "x_far")
    x_far_other = along_col(x_above, col_perm(0, -1, 1), "x_far_other")

    (y_below,) = after([y_below], [zl_below])
    y_far, zl_far = along_row(y_below, y_up, "y_far"), along_row(zl_above, y_down, "zl_far")
    again, x_below, x_above = after([again, x_below, x_above], [zl_below, zl_above, zh, x_far, x_far_other])
    swaps = [along_col(block, flip, "core_swap") for block in (again, x_below, x_above)]
    zh, x_far = after([zh, x_far], swaps)
    zh_below, zh_above = along_col(zh, x_up, "zh_below"), along_col(zh, x_down, "zh_above")
    zh_far = along_col(x_far, col_perm(1, 0, 0), "zh_far")

    second = [own, y_below, y_above, y_far, zl, zl_below, zl_above, zl_far]
    table = lag_table()
    blocks = [own, x_below, x_above, x_far, *swaps, x_far_other]
    result = pair_chunk(blocks, places[0], second, scale, table, None)
    blocks = after([zh, zh_below, zh_above, zh_far], [result])
    blocks = [*blocks, *(along_col(block, flip, "core_swap") for block in blocks)]
    result = pair_chunk(blocks, places[1], second, scale, table, result)
    return result


def solution(mesh):
    placed = (P(None, ("row", "col")), P(), P())
    return jax.shard_map(
        per_device, mesh=mesh, in_specs=placed, out_specs=P("row", "col", None), check_vma=False
    )
```
